32 devices in a mesh: leaf: 8 (over z, y), probe: 4 (over x, core).
Axes of the slice: x: 2, y: 2, z: 4, core: 2. Of those that a mesh axis runs over, the one named last changes fastest.
Arguments:
- coords: float32 [3, 32768], P(None, 'leaf'), may hold values from 0 to 1
- weights: float32 [32768], P('leaf'), may hold values from 0.01 to 0.1
- omega: bfloat16 [256, 32768], P('probe', 'leaf'), may hold values from -6 to 6
- near_local: int32 [256, 24], P('leaf'), may hold values from 0 to 255, as said below
- far_pairs: int32 [2, 512], P(None, 'leaf'), may hold values from 0 to 255, as said below
- skel_rows: int32 [256, 32], P('leaf'), may hold values from 0 to 127, as said below
- parent_interp: bfloat16 [32, 256, 64], P('leaf'), may hold values from -0.375 to 0.375
Outputs:
- near_sample: float32 [256, 32768], P('probe', 'leaf')
- parent_sample: float32 [256, 2048], P('probe', 'leaf')
The draws below stay inside these ranges and needn't reach their ends.
Inputs may be any that keep to these rules, and one draw needn't show every extreme that they name: `near_local`: entry 0 of leaf t's row is t itself; every other entry names a leaf of the same device as t (equal index // 32); repeats may occur. `far_pairs`: column c belongs to device c // 64: its source leaf lies on that device and its target leaf on another device. Of one device's 64 columns at most 16 have targets on any one other device, and one device receives exactly 16 from every other device. `skel_rows`: the 32 numbers of one leaf are distinct.
All inputs are finite; a program needn't handle non-finite values.
Results may differ from the reference program's by a relative error of at most 0.008.
Values may be sent and summed in bfloat16 or wider, within the bound.
No kernel may reach another device: no remote copies, remote signals or barrier semaphores. Data moves between devices by JAX's collectives and lax.ppermute only.
A program may use at most 64 MiB of HBM per device.

```python
import math
import jax
import jax.numpy as jnp
from jax import lax

LEAF_PTS = 128
PROBES = 256
SK = 32
SK2 = 64
CHILD = 8
NLOC = 24
CAP = 16
LEAF_DEV = 32
LEAVES = 256
BOUNDARY_NODES = 32768
PARENTS = 32
REMOTE_DEV = 64
N_LEAF = 8


def draw_near_local(key, part):
    leaf_rows = jnp.arange(LEAVES, dtype=jnp.int32)
    leaf_base = leaf_rows // LEAF_DEV * LEAF_DEV
    others = jax.random.randint(key, (LEAVES, NLOC - 1), 0, LEAF_DEV, dtype=jnp.int32)
    return jnp.concatenate([leaf_rows[:, None], leaf_base[:, None] + others], axis=1)


def draw_far_pairs(key, part):
    device_count = LEAVES // LEAF_DEV
    hot_device = jax.random.randint(jax.random.fold_in(key, 7), (), 0, device_count, dtype=jnp.int32)
    labels = jnp.arange((device_count - 1) * CAP, dtype=jnp.int32) // CAP

    def per_device(device):
        subkey = jax.random.fold_in(key, device + 11)
        key_one, key_two, key_three, key_four = jax.random.split(subkey, 4)
        peer_dev = (device + 1 + labels) % device_count
        scores = jax.random.permutation(key_one, labels.shape[0]).astype(jnp.int32)
        scores = jnp.where(peer_dev == hot_device, scores - labels.shape[0], scores)
        ranked = jnp.argsort(scores, stable=True)[:REMOTE_DEV]
        chosen = jax.random.permutation(key_two, peer_dev[ranked])
        target = chosen * LEAF_DEV + jax.random.randint(key_three, (REMOTE_DEV,), 0, LEAF_DEV, dtype=jnp.int32)
        source = device * LEAF_DEV + jax.random.randint(key_four, (REMOTE_DEV,), 0, LEAF_DEV, dtype=jnp.int32)
        return jnp.stack([source, target])
    pairs = jax.vmap(per_device)(jnp.arange(device_count, dtype=jnp.int32))
    return pairs.transpose(1, 0, 2).reshape(2, device_count * REMOTE_DEV)


def draw_skel_rows(key, part):
    leaf_random_keys = jax.random.split(key, LEAVES)

    def per_leaf(leaf_key):
        return jax.random.permutation(leaf_key, LEAF_PTS)[:SK].astype(jnp.int32)
    return jax.vmap(per_leaf)(leaf_random_keys)


def level_of(key, extent, shards, low, top_value):
    level = 1.0
    for position, parts in shards:
        heights = jax.random.uniform(jax.random.fold_in(jax.random.fold_in(key, 6), position), (parts,), jnp.float32, low / len(shards), top_value / len(shards))
        level = level * jnp.repeat(jnp.exp(heights), extent[position] // parts).reshape((-1,) + (1,) * (len(extent) - 1 - position))
    return level


def normal_values(key, extent, width, reach, pieces=(), kind=jnp.bfloat16):
    entries = jax.random.normal(key, extent, jnp.float32) * width
    if len(pieces) > 0:
        entries = level_of(key, extent, pieces, -0.22, 0.18) * entries
    return jnp.clip(entries, min=-reach, max=reach).astype(kind)


def setup_inputs(seed: int = 0) -> dict:
    seeds = jax.random.split(jax.random.key(seed), 8)
    return {
        "coords": jnp.clip(1.0 * jax.random.uniform(seeds[0], (3, BOUNDARY_NODES), jnp.float32) ** level_of(seeds[0], (3, BOUNDARY_NODES), ((1, 8),), -0.2, 0.2), 0.0, 1.0),
        "weights": jnp.clip(jnp.exp(math.log(0.1) - 2.3025851 * jax.random.uniform(seeds[1], (BOUNDARY_NODES,), jnp.float32) ** level_of(seeds[1], (BOUNDARY_NODES,), ((0, 8),), -0.2, 0.2)), 0.01, 0.1),
        "omega": normal_values(seeds[2], (PROBES, BOUNDARY_NODES), 1.0, 6.0, ((0, 4), (1, 8))),
        "near_local": draw_near_local(jax.random.fold_in(seeds[7], 71), 0),
        "far_pairs": draw_far_pairs(jax.random.fold_in(seeds[7], 71), 0),
        "skel_rows": draw_skel_rows(jax.random.fold_in(seeds[7], 71), 0),
        "parent_interp": normal_values(seeds[6], (PARENTS, CHILD * SK, SK2), (CHILD * SK) ** -0.5, 0.375, ((0, 8),)),
    }


DELTA_SQ = 0.0001
INV_FOUR_PI = 0.07957747154594767

def kernel_block(target_points, source_points, source_weights):
    delta_x = target_points[..., 0, :, None] - source_points[..., 0, None, :]
    delta_y = target_points[..., 1, :, None] - source_points[..., 1, None, :]
    delta_z = target_points[..., 2, :, None] - source_points[..., 2, None, :]
    dist_sq = delta_x * delta_x + delta_y * delta_y + delta_z * delta_z
    values = source_weights[..., None, :] * INV_FOUR_PI * lax.rsqrt(dist_sq + DELTA_SQ)
    return values.astype(jnp.bfloat16)

def reference(coords, weights, omega, near_local, far_pairs, skel_rows, parent_interp):
    leaf_node_coords = coords.reshape(3, LEAVES, LEAF_PTS).transpose(1, 0, 2)
    leaf_weights = weights.reshape(LEAVES, LEAF_PTS)
    leaf_probes = omega.reshape(PROBES, LEAVES, LEAF_PTS).transpose(1, 0, 2)
    block_size = 8

    def local_block(first_leaf):
        targets = lax.dynamic_slice_in_dim(leaf_node_coords, first_leaf, block_size, 0)
        sources = lax.dynamic_slice_in_dim(near_local, first_leaf, block_size, 0)
        kernel = kernel_block(targets[:, None], leaf_node_coords[sources], leaf_weights[sources])
        kernel = lax.optimization_barrier(kernel).astype(jnp.float32)
        return jnp.einsum('bjts,bjps->bpt', kernel, leaf_probes[sources].astype(jnp.float32))
    firsts = jnp.arange(0, LEAVES, block_size, dtype=jnp.int32)
    local_sum = lax.map(local_block, firsts).reshape(LEAVES, PROBES, LEAF_PTS)

    def remote_loop_body(device, total):
        first_pair = (device * REMOTE_DEV).astype(jnp.int32)
        pairs = lax.dynamic_slice_in_dim(far_pairs, first_pair, REMOTE_DEV, 1)
        source = pairs[0]
        target = pairs[1]
        kernel = kernel_block(leaf_node_coords[target], leaf_node_coords[source], leaf_weights[source])
        kernel = lax.optimization_barrier(kernel).astype(jnp.float32)
        partial_rows = jnp.einsum('nts,nps->npt', kernel, leaf_probes[source].astype(jnp.float32))
        partial_rows = lax.optimization_barrier(partial_rows.astype(jnp.bfloat16)).astype(jnp.float32)
        return total.at[target].add(partial_rows)
    far_sum = lax.fori_loop(0, N_LEAF, remote_loop_body, jnp.zeros((LEAVES, PROBES, LEAF_PTS), jnp.float32))
    sampled_block = local_sum + far_sum
    near_sample = sampled_block.transpose(1, 0, 2).reshape(PROBES, BOUNDARY_NODES)
    index_rows = jnp.broadcast_to(skel_rows[:, None, :], (LEAVES, PROBES, SK))
    selected_entries = jnp.take_along_axis(sampled_block, index_rows, axis=2).astype(jnp.bfloat16)
    selected_entries = lax.optimization_barrier(selected_entries).astype(jnp.float32)
    stacked = selected_entries.reshape(PARENTS, CHILD, PROBES, SK).transpose(0, 2, 1, 3).reshape(PARENTS, PROBES, CHILD * SK)
    merged = jnp.einsum('pqc,pck->pqk', stacked, parent_interp.astype(jnp.float32))
    energy = lax.optimization_barrier(jnp.sum(merged * merged, axis=(1, 2)))
    factor = lax.rsqrt(energy / (SK2 * PROBES) + 1e-06)
    parent_sample = (merged * factor[:, None, None]).transpose(1, 0, 2).reshape(PROBES, PARENTS * SK2)
    return (near_sample, parent_sample)
```

```python
import functools

import jax
import jax.numpy as jnp
from jax import lax
from jax.experimental import pallas as pl
from jax.experimental.pallas import tpu as pltpu
from jax.sharding import PartitionSpec as P

LEAF_PTS = 128
SK = 32
SK2 = 64
CHILD = 8

DELTA_SQ = 0.0001
INV_FOUR_PI = 0.07957747154594767

VMEM_LIMIT = 48 * 1024 * 1024
GROUP = 4

SMEM = pl.BlockSpec(memory_space=pltpu.SMEM)
VMEM = pl.BlockSpec(memory_space=pltpu.VMEM)


def leaf_lanes(leaf):
    return pl.ds(pl.multiple_of(leaf * LEAF_PTS, LEAF_PTS), LEAF_PTS)


def column_of(row):
    return jnp.transpose(jnp.broadcast_to(row, (LEAF_PTS, LEAF_PTS)))


def kernel_block(columns, source, scale):
    delta_x = columns[0] - source[0:1]
    delta_y = columns[1] - source[1:2]
    delta_z = columns[2] - source[2:3]
    dist_sq = delta_x * delta_x + delta_y * delta_y + delta_z * delta_z
    values = source[3:4] * scale * lax.rsqrt(dist_sq + DELTA_SQ)
    return values.astype(jnp.bfloat16)


def times_block(probes, block):
    return lax.dot_general(
        probes, block, (((1,), (1,)), ((), ())), preferred_element_type=jnp.float32
    )


def local_body(index_ref, count_ref, groups_ref, points_ref, omega_ref, out_ref, cols_ref):
    leaf_dev = groups_ref.shape[0]

    def target_step(t, carry):
        for c in range(3):
            cols_ref[c] = column_of(points_ref[c : c + 1, leaf_lanes(t)])

        def group_step(g, total):
            for u in range(GROUP):
                s = index_ref[t, g * GROUP + u]
                scale = count_ref[t, g * GROUP + u] * INV_FOUR_PI
                source = points_ref[:, leaf_lanes(s)]
                block = kernel_block([cols_ref[c] for c in range(3)], source, scale)
                total = total + times_block(omega_ref[:, leaf_lanes(s)], block)
            return total

        zero = jnp.zeros((omega_ref.shape[0], LEAF_PTS), jnp.float32)
        out_ref[:, leaf_lanes(t)] = lax.fori_loop(0, groups_ref[t], group_step, zero)
        return carry

    lax.fori_loop(0, leaf_dev, target_step, 0)


def far_body(dests, *refs):
    source_ref, target_ref = refs[:2]
    target_points = refs[2 : 2 + dests]
    source_points = refs[2 + dests : 6 + dests]
    omegas = refs[6 + dests : 10 + dests]
    own_ref = refs[10 + dests]
    rest_ref = refs[11 + dests]
    total_ref, cols_ref = refs[12 + dests :]
    leaf_dev = own_ref.shape[1] // LEAF_PTS
    pairs = source_ref.shape[1]
    total_ref[...] = jnp.zeros_like(total_ref)
    for k in range(4):

        def pair_step(p, carry, k=k):
            target = target_ref[k, p]

            @pl.when(target >= 0)
            def _():
                s = source_ref[k, p]
                leaf = lax.rem(target, leaf_dev)
                dest = lax.div(target, leaf_dev)
                for r in range(dests):

                    @pl.when(dest == r)
                    def _(r=r):
                        for c in range(3):
                            cols_ref[c] = column_of(target_points[r][c : c + 1, leaf_lanes(leaf)])

                source = source_points[k][:, leaf_lanes(s)]
                block = kernel_block([cols_ref[c] for c in range(3)], source, INV_FOUR_PI)
                total_ref[dest, :, leaf_lanes(leaf)] += times_block(
                    omegas[k][:, leaf_lanes(s)], block
                )

            return carry

        lax.fori_loop(0, pairs, pair_step, 0)
    own_ref[...] = total_ref[0]
    for r in range(1, dests):
        rest_ref[r - 1] = total_ref[r].astype(jnp.bfloat16)


def merge_body(local_ref, own_ref, arrived_ref, pick_ref, near_ref, merged_ref, energy_ref):
    near = local_ref[...] + own_ref[...] + arrived_ref[...].astype(jnp.float32)
    near_ref[...] = near
    rounded = near.astype(jnp.bfloat16)
    parents, width, _ = pick_ref.shape
    for p in range(parents):
        merged = jnp.dot(
            rounded[:, p * width : (p + 1) * width], pick_ref[p], preferred_element_type=jnp.float32
        )
        merged_ref[:, p * SK2 : (p + 1) * SK2] = merged
        energy_ref[p : p + 1, :] = jnp.broadcast_to(
            jnp.sum(jnp.sum(merged * merged, axis=0, keepdims=True), axis=1, keepdims=True),
            (1, LEAF_PTS),
        )


def scale_body(count, merged_ref, energy_ref, out_ref):
    parents = energy_ref.shape[0]
    for p in range(parents):
        factor = lax.rsqrt(energy_ref[p : p + 1, 0:SK2] / count + 1e-06)
        out_ref[:, p * SK2 : (p + 1) * SK2] = merged_ref[:, p * SK2 : (p + 1) * SK2] * factor


def call(body, out_shape, in_specs, scratch=()):
    many = isinstance(out_shape, (tuple, list))
    return pl.pallas_call(
        body,
        out_shape=out_shape,
        in_specs=in_specs,
        out_specs=[VMEM] * len(out_shape) if many else VMEM,
        scratch_shapes=list(scratch),
        compiler_params=pltpu.CompilerParams(vmem_limit_bytes=VMEM_LIMIT),
    )


def exchange(array, axis, bit):
    size = lax.axis_size(axis)
    return lax.ppermute(array, axis, [(i, i ^ bit) for i in range(size)])


def local_tables(near_local, offset, leaf_dev):
    leaf_iota = jnp.arange(leaf_dev, dtype=jnp.int32)
    ids = near_local - offset
    counts = jnp.sum((ids[:, :, None] == leaf_iota).astype(jnp.int32), axis=1)
    present = (counts > 0).astype(jnp.int32)
    before = (leaf_iota[:, None] < leaf_iota[None, :]).astype(jnp.int32)
    place = jnp.sum(present[:, :, None] * before[None], axis=1)
    hit = (place[:, :, None] == leaf_iota).astype(jnp.int32) * present[:, :, None]
    index = jnp.sum(hit * leaf_iota[None, :, None], axis=1)
    count = jnp.sum(hit * counts[:, :, None], axis=1).astype(jnp.float32)
    groups = (jnp.sum(present, axis=1) + GROUP - 1) // GROUP
    return index, count, groups


def per_device(coords, weights, omega, near_local, far_pairs, skel_rows, parent_interp):
    n_leaf = lax.axis_size("leaf")
    points = coords.shape[1]
    leaf_dev = points // LEAF_PTS
    probe_dev = omega.shape[0]
    parent_dev = leaf_dev // CHILD
    me = lax.axis_index("leaf")
    top, low = n_leaf // 2, 1
    dests = n_leaf // 4
    pair_dev = far_pairs.shape[1]

    bundle = jnp.concatenate([coords, weights[None]], axis=0)
    pair_columns = 2 * pair_dev // 4
    sent = jnp.concatenate(
        [bundle, far_pairs.reshape(4, pair_columns).astype(jnp.float32)], axis=1
    )
    across = exchange(sent, "leaf", top)
    beside = exchange(sent, "leaf", low)
    target_bundles = [bundle] + [
        exchange(bundle, "leaf", 2 * r) for r in range(1, dests)
    ]
    both = exchange(across, "leaf", low)
    omega_across = exchange(omega, "leaf", top)
    omega_beside = exchange(omega, "leaf", low)
    omega_both = exchange(omega_across, "leaf", low)

    index, count, groups = local_tables(near_local, me * leaf_dev, leaf_dev)
    local = call(
        local_body,
        jax.ShapeDtypeStruct((probe_dev, points), jnp.float32),
        [SMEM, SMEM, SMEM, VMEM, VMEM],
        [pltpu.VMEM((3, LEAF_PTS, LEAF_PTS), jnp.float32)],
    )(index, count, groups, bundle, omega)

    bundles = [sent, across, beside, both]
    pairs = jnp.stack([b[:, points:].astype(jnp.int32).reshape(2, pair_dev) for b in bundles])
    owners = me ^ jnp.array([0, top, low, top | low], jnp.int32)
    sources = pairs[:, 0] - owners[:, None] * leaf_dev
    relation = (pairs[:, 1] // leaf_dev) ^ me
    inside = (relation & (top | low)) == 0
    targets = jnp.where(inside, (relation // 2) * leaf_dev + pairs[:, 1] % leaf_dev, -1)
    own, rest = call(
        functools.partial(far_body, dests),
        [
            jax.ShapeDtypeStruct((probe_dev, points), jnp.float32),
            jax.ShapeDtypeStruct((dests - 1, probe_dev, points), jnp.bfloat16),
        ],
        [SMEM, SMEM] + [VMEM] * (dests + 8),
        [
            pltpu.VMEM((dests, probe_dev, points), jnp.float32),
            pltpu.VMEM((3, LEAF_PTS, LEAF_PTS), jnp.float32),
        ],
    )(
        sources,
        targets,
        *target_bundles,
        *bundles,
        omega,
        omega_across,
        omega_beside,
        omega_both,
    )
    half = dests // 2
    while half > 1:
        got = exchange(rest[half - 1 :], "leaf", 2 * half)
        own = own + got[0].astype(jnp.float32)
        rest = rest[: half - 1] + got[1:]
        half //= 2
    arrived = exchange(rest[0], "leaf", 2)

    rows = (
        jnp.arange(LEAF_PTS, dtype=jnp.int32)[None, :, None] == skel_rows[:, None, :]
    ).astype(jnp.bfloat16)
    weights_of = parent_interp.reshape(leaf_dev, SK, SK2)
    pick = jnp.einsum("lir,lrk->lik", rows, weights_of, preferred_element_type=jnp.float32)
    pick = pick.astype(jnp.bfloat16).reshape(parent_dev, CHILD * LEAF_PTS, SK2)
    near, merged, energy = call(
        merge_body,
        [
            jax.ShapeDtypeStruct((probe_dev, points), jnp.float32),
            jax.ShapeDtypeStruct((probe_dev, parent_dev * SK2), jnp.float32),
            jax.ShapeDtypeStruct((parent_dev, LEAF_PTS), jnp.float32),
        ],
        [VMEM] * 4,
    )(local, own, arrived, pick)
    energy = lax.psum(energy, "probe")
    parent = call(
        functools.partial(scale_body, float(SK2 * probe_dev * lax.axis_size("probe"))),
        jax.ShapeDtypeStruct((probe_dev, parent_dev * SK2), jnp.float32),
        [VMEM] * 2,
    )(merged, energy)
    return near, parent


def solution(mesh):
    return jax.shard_map(
        per_device,
        mesh=mesh,
        in_specs=(
            P(None, "leaf"),
            P("leaf"),
            P("probe", "leaf"),
            P("leaf", None),
            P(None, "leaf"),
            P("leaf", None),
            P("leaf", None, None),
        ),
        out_specs=(P("probe", "leaf"), P("probe", "leaf")),
        check_vma=False,
    )
```

```python
import functools

import jax
import jax.numpy as jnp
from jax import lax
from jax.experimental import pallas as pl
from jax.experimental.pallas import tpu as pltpu
from jax.sharding import PartitionSpec as P

LEAF_PTS = 128
SK = 32
SK2 = 64
CHILD = 8
CAP = 16

DELTA_SQ = 0.0001
INV_FOUR_PI = 0.07957747154594767

VMEM_LIMIT = 12 * 1024 * 1024
BATCH = 8
FEATURES = 32
CHUNKS = (1, 1)
LOCAL_PARTS = 1

SMEM = pl.BlockSpec(memory_space=pltpu.SMEM)
VMEM = pl.BlockSpec(memory_space=pltpu.VMEM)


def leaf_range(leaf):
    return pl.ds(pl.multiple_of(leaf * LEAF_PTS, LEAF_PTS), LEAF_PTS)


def split_three(values):
    first = values.astype(jnp.bfloat16).astype(jnp.float32)
    rest = values - first
    second = rest.astype(jnp.bfloat16).astype(jnp.float32)
    return first, second, rest - second


def six_products(left, right):
    a, b, c = split_three(left)
    p, q, r = split_three(right)
    return (a, a, b, b, a, c), (p, q, p, q, r, p)


def feature_body(n_source, n_target, *refs):
    source_ref, target_ref, rows = refs[n_source + n_target :]
    points = rows.shape[1]
    rows[27:FEATURES, :] = jnp.zeros((FEATURES - 27, points), jnp.float32)
    for i in range(n_source + n_target):
        points_ref = refs[i]
        centred = points_ref[0:3, :points] - 0.5
        square = centred * centred
        norm = square[0:1] + square[1:2] + square[2:3]
        if i < n_source:
            root = 1.0 / (points_ref[3:4, :points] * INV_FOUR_PI)
            scale = root * root
            side, shared, last = 1, (centred * scale, scale), scale * (norm + DELTA_SQ)
            out = source_ref.at[:, i * points : (i + 1) * points]
        else:
            side, shared, last = 0, (-2.0 * centred, norm), None
            out = target_ref.at[:, (i - n_source) * points : (i - n_source + 1) * points]
        first = 0
        for values in shared:
            for part in six_products(values, values)[side]:
                rows[first : first + values.shape[0], :] = part
                first += values.shape[0]
        parts = [jnp.ones_like(norm)] * 3 if last is None else split_three(last)
        for part in parts:
            rows[first : first + 1, :] = part
            first += 1
        out[...] = rows[...].astype(jnp.bfloat16)


def turned_block(source, target):
    scaled = lax.dot_general(
        source, target, (((0,), (0,)), ((), ())), preferred_element_type=jnp.float32
    )
    return lax.rsqrt(scaled).astype(jnp.bfloat16)


def local_body(
    first, offset_ref, near_ref, target_ref, source_ref, omega_ref, out_ref, even_ref, odd_ref
):
    entries = near_ref.shape[1]
    leaves = out_ref.shape[1] // LEAF_PTS
    offset = offset_ref[0]

    def source_of(t, e):
        return leaf_range(near_ref[first + t, e] - offset)

    def make(t, block_ref):
        target = target_ref[:, leaf_range(first + t)]
        for e in range(entries):
            block_ref[e * LEAF_PTS : (e + 1) * LEAF_PTS, :] = turned_block(
                source_ref[:, source_of(t, e)], target
            )

    def use(t, block_ref):
        probes = jnp.concatenate([omega_ref[:, source_of(t, e)] for e in range(entries)], axis=1)
        out_ref[:, leaf_range(t)] = jnp.dot(
            probes, block_ref[...], preferred_element_type=jnp.float32
        )

    make(0, even_ref)

    def step(k, carry):
        make(2 * k + 1, odd_ref)
        use(2 * k, even_ref)
        make(jnp.minimum(2 * k + 2, leaves - 1), even_ref)
        use(2 * k + 1, odd_ref)
        return carry

    lax.fori_loop(0, leaves // 2, step, 0)


def far_body(first, count_ref, table_ref, source_ref, target_ref, *refs):
    omegas = refs[:4]
    own_ref, rest_ref, even_ref, odd_ref, total_ref, omega_ref = refs[4:]
    size, points = own_ref.shape
    count = count_ref[0]
    total_ref[...] = jnp.zeros_like(total_ref)
    for k in range(4):
        cut = slice(k * points, (k + 1) * points)
        rows = slice(first, first + size) if k < 3 else slice(0, size)
        omega_ref[:, cut] = omegas[k][rows, :]

    def make(base, block_ref):
        for u in range(BATCH):
            block_ref[u] = turned_block(
                source_ref[:, leaf_range(table_ref[0, base + u])],
                target_ref[:, leaf_range(table_ref[1, base + u])],
            )

    def use(base, block_ref):
        for u in range(BATCH):
            product = jnp.dot(
                omega_ref[:, leaf_range(table_ref[0, base + u])],
                block_ref[u],
                preferred_element_type=jnp.float32,
            )
            total_ref[:, leaf_range(table_ref[1, base + u])] += jnp.where(
                base + u < count, product, 0.0
            )

    make(0, even_ref)

    def step(k, carry):
        make((2 * k + 1) * BATCH, odd_ref)
        use(2 * k * BATCH, even_ref)
        make((2 * k + 2) * BATCH, even_ref)
        use((2 * k + 1) * BATCH, odd_ref)
        return carry

    lax.fori_loop(0, lax.div(count + 2 * BATCH - 1, 2 * BATCH), step, 0)
    own_ref[...] = total_ref[:, :points]
    for r in range(1, rest_ref.shape[0] + 1):
        rest_ref[r - 1] = total_ref[:, r * points : (r + 1) * points].astype(jnp.bfloat16)


def pick_body(skel_ref, interp_ref, out_ref):
    turned = jnp.transpose(skel_ref[...].astype(jnp.float32)).astype(jnp.int32)
    lane = lax.broadcasted_iota(jnp.int32, (SK, LEAF_PTS), 1)
    for leaf in range(skel_ref.shape[0]):
        parent, child = divmod(leaf, CHILD)
        chosen = (turned[:, leaf : leaf + 1] == lane).astype(jnp.float32).astype(jnp.bfloat16)
        out_ref[parent, :, child * LEAF_PTS : (child + 1) * LEAF_PTS] = jnp.dot(
            interp_ref[parent, :, child * SK : (child + 1) * SK],
            chosen,
            preferred_element_type=jnp.float32,
        ).astype(jnp.bfloat16)


def merge_body(n_local, n_chunk, *refs):
    locals_ = refs[:n_local]
    owns = refs[n_local : n_local + n_chunk]
    arrived = refs[n_local + n_chunk : n_local + 2 * n_chunk]
    pick_ref, near_ref, merged_ref, energy_ref = refs[n_local + 2 * n_chunk :]
    width = locals_[0].shape[1]
    for i in range(n_local):
        columns = slice(i * width, (i + 1) * width)
        first = 0
        for own_ref, arrived_ref in zip(owns, arrived):
            rows = slice(first, first + own_ref.shape[0])
            first += own_ref.shape[0]
            near_ref[rows, columns] = (
                locals_[i][rows, :]
                + own_ref[:, columns]
                + arrived_ref[:, columns].astype(jnp.float32)
            )
    parents, _, width = pick_ref.shape
    for p in range(parents):
        merged = lax.dot_general(
            near_ref[:, p * width : (p + 1) * width].astype(jnp.bfloat16),
            pick_ref[p],
            (((1,), (1,)), ((), ())),
            preferred_element_type=jnp.float32,
        )
        merged_ref[:, p * SK2 : (p + 1) * SK2] = merged
        energy_ref[p : p + 1, :] = jnp.broadcast_to(
            jnp.sum(jnp.sum(merged * merged, axis=0, keepdims=True), axis=1, keepdims=True),
            (1, LEAF_PTS),
        )


def scale_body(count, merged_ref, energy_ref, out_ref):
    parents = energy_ref.shape[0]
    for p in range(parents):
        factor = lax.rsqrt(energy_ref[p : p + 1, 0:SK2] / count + 1e-06)
        out_ref[:, p * SK2 : (p + 1) * SK2] = merged_ref[:, p * SK2 : (p + 1) * SK2] * factor


def call(body, out_shape, in_specs, scratch=(), micros=1.0):
    many = isinstance(out_shape, (tuple, list))
    return pl.pallas_call(
        body,
        out_shape=out_shape,
        in_specs=in_specs,
        out_specs=[VMEM] * len(out_shape) if many else VMEM,
        scratch_shapes=list(scratch),
        compiler_params=pltpu.CompilerParams(vmem_limit_bytes=VMEM_LIMIT),
        cost_estimate=pl.CostEstimate(
            flops=int(micros * 1e7), bytes_accessed=int(micros * 3e4), transcendentals=0
        ),
    )


def features_of(points, sources, targets):
    return call(
        functools.partial(feature_body, len(sources), len(targets)),
        [
            jax.ShapeDtypeStruct((FEATURES, len(sources) * points), jnp.bfloat16),
            jax.ShapeDtypeStruct((FEATURES, len(targets) * points), jnp.bfloat16),
        ],
        [VMEM] * (len(sources) + len(targets)),
        [pltpu.VMEM((FEATURES, points), jnp.float32)],
    )(*sources, *targets)


def exchange(array, axis, bit):
    size = lax.axis_size(axis)
    return lax.ppermute(array, axis, [(i, i ^ bit) for i in range(size)])


def after(array, *others):
    return lax.optimization_barrier((array, *others))[0]


def far_table(pairs, me, masks, outer, leaf_dev, length):
    owners = me ^ jnp.array(masks, jnp.int32)
    source = pairs[:, 0] - owners[:, None] * leaf_dev
    source += jnp.arange(4, dtype=jnp.int32)[:, None] * leaf_dev
    relation = (pairs[:, 1] // leaf_dev) ^ me
    inside = ((relation & outer) == 0).reshape(-1)
    target = (relation // 2) * leaf_dev + pairs[:, 1] % leaf_dev
    iota = jnp.arange(inside.shape[0], dtype=jnp.int32)
    place = jnp.sum(
        (inside[:, None] & (iota[:, None] < iota[None, :])).astype(jnp.int32), axis=0
    )
    place = jnp.where(inside, place, -1)
    hit = place[None, None, :] == jnp.arange(length, dtype=jnp.int32)[None, :, None]
    codes = jnp.stack([source.reshape(-1), target.reshape(-1)])
    return (
        jnp.sum(inside.astype(jnp.int32)).reshape(1),
        jnp.sum(jnp.where(hit, codes[:, None, :], 0), axis=2),
    )


def per_device(coords, weights, omega, near_local, far_pairs, skel_rows, parent_interp):
    n_leaf = lax.axis_size("leaf")
    points = coords.shape[1]
    leaf_dev = points // LEAF_PTS
    probe_dev = omega.shape[0]
    parent_dev = leaf_dev // CHILD
    me = lax.axis_index("leaf")
    top, low = n_leaf // 2, 1
    dests = n_leaf // 4
    pair_dev = far_pairs.shape[1]
    unit = probe_dev // sum(CHUNKS)
    chunks = [(unit * sum(CHUNKS[:i]), unit * c) for i, c in enumerate(CHUNKS)]

    omega_across = exchange(omega, "leaf", top)
    pair_columns = 2 * pair_dev // 4
    sent = jnp.concatenate(
        [
            jnp.concatenate([coords, weights[None]], axis=0),
            far_pairs.reshape(4, pair_columns).astype(jnp.float32),
        ],
        axis=1,
    )
    across = exchange(sent, "leaf", top)

    source, target = features_of(points, [sent], [sent])
    part_points = points // LOCAL_PARTS
    entries = near_local.shape[1]

    def local_part(i, table):
        return call(
            functools.partial(local_body, i * part_points // LEAF_PTS),
            jax.ShapeDtypeStruct((probe_dev, part_points), jnp.float32),
            [SMEM, SMEM, VMEM, VMEM, VMEM],
            [pltpu.VMEM((entries * LEAF_PTS, LEAF_PTS), jnp.bfloat16)] * 2,
            micros=16.0 / LOCAL_PARTS,
        )((me * leaf_dev).reshape(1), table, target, source, omega)

    omega_beside = exchange(omega, "leaf", low)
    beside = exchange(sent, "leaf", low)
    partners = [exchange(sent, "leaf", 2 * r) for r in range(1, dests)]
    both = exchange(across, "leaf", low)
    local = [local_part(i, near_local) for i in range(LOCAL_PARTS)]
    omega_across = after(omega_across, *local)
    relayed = []
    for first, size in chunks:
        part = omega_across[first : first + size]
        if relayed:
            part = after(omega_across, relayed[-1])[first : first + size]
        relayed.append(exchange(part, "leaf", low))

    bundles = [sent, across, beside, both]
    pairs = jnp.stack([b[:, points:].astype(jnp.int32).reshape(2, pair_dev) for b in bundles])
    pairs = after(pairs, omega_across)
    rounds = (dests * 4 * CAP + 2 * BATCH - 1) // (2 * BATCH)
    far_count, codes = far_table(
        pairs, me, [0, top, low, top | low], top | low, leaf_dev, (2 * rounds + 1) * BATCH
    )
    far_source, far_target = features_of(points, bundles, [sent, *partners])
    owns, arrived = [], []
    for (first, size), omega_both in zip(chunks, relayed):
        own, rest = call(
            functools.partial(far_body, first),
            [
                jax.ShapeDtypeStruct((size, points), jnp.float32),
                jax.ShapeDtypeStruct((dests - 1, size, points), jnp.bfloat16),
            ],
            [SMEM, SMEM] + [VMEM] * 6,
            [
                pltpu.VMEM((BATCH, LEAF_PTS, LEAF_PTS), jnp.bfloat16),
                pltpu.VMEM((BATCH, LEAF_PTS, LEAF_PTS), jnp.bfloat16),
                pltpu.VMEM((size, dests * points), jnp.float32),
                pltpu.VMEM((size, 4 * points), jnp.bfloat16),
            ],
            micros=4.0,
        )(
            far_count, codes, far_source, far_target, omega, omega_across, omega_beside, omega_both
        )
        half = dests // 2
        while half > 1:
            got = exchange(rest[half - 1 :], "leaf", 2 * half)
            own = own + got[0].astype(jnp.float32)
            rest = rest[: half - 1] + got[1:]
            half //= 2
        owns.append(own)
        arrived.append(exchange(rest[0], "leaf", 2))
    pick = call(
        pick_body,
        jax.ShapeDtypeStruct((parent_dev, SK2, CHILD * LEAF_PTS), jnp.bfloat16),
        [VMEM] * 2,
    )(skel_rows, parent_interp.transpose(0, 2, 1))
    near, merged, energy = call(
        functools.partial(merge_body, LOCAL_PARTS, len(chunks)),
        [
            jax.ShapeDtypeStruct((probe_dev, points), jnp.float32),
            jax.ShapeDtypeStruct((probe_dev, parent_dev * SK2), jnp.float32),
            jax.ShapeDtypeStruct((parent_dev, LEAF_PTS), jnp.float32),
        ],
        [VMEM] * (LOCAL_PARTS + 2 * len(chunks) + 1),
        micros=2.0,
    )(*local, *owns, *arrived, pick)
    energy = lax.psum(energy, "probe")
    parent = call(
        functools.partial(scale_body, float(SK2 * probe_dev * lax.axis_size("probe"))),
        jax.ShapeDtypeStruct((probe_dev, parent_dev * SK2), jnp.float32),
        [VMEM] * 2,
    )(merged, energy)
    return near, parent


def solution(mesh):
    return jax.shard_map(
        per_device,
        mesh=mesh,
        in_specs=(
            P(None, "leaf"),
            P("leaf"),
            P("probe", "leaf"),
            P("leaf", None),
            P(None, "leaf"),
            P("leaf", None),
            P("leaf", None, None),
        ),
        out_specs=(P("probe", "leaf"), P("probe", "leaf")),
        check_vma=False,
    )
```

```python
import functools

import jax
import jax.numpy as jnp
from jax import lax
from jax.experimental import pallas as pl
from jax.experimental.pallas import tpu as pltpu
from jax.sharding import PartitionSpec as P

LEAF_PTS = 128
SK = 32
SK2 = 64
CHILD = 8
CAP = 16

DELTA_SQ = 0.0001
INV_FOUR_PI = 0.07957747154594767

VMEM_LIMIT = 12 * 1024 * 1024
BATCH = 24
FEATURES = 32
CHUNKS = (1, 1)
LOCAL_PARTS = 1

SMEM = pl.BlockSpec(memory_space=pltpu.SMEM)
VMEM = pl.BlockSpec(memory_space=pltpu.VMEM)
HBM = pl.BlockSpec(memory_space=pltpu.HBM)


def leaf_range(leaf):
    return pl.ds(pl.multiple_of(leaf * LEAF_PTS, LEAF_PTS), LEAF_PTS)


def split_three(values):
    first = values.astype(jnp.bfloat16).astype(jnp.float32)
    rest = values - first
    second = rest.astype(jnp.bfloat16).astype(jnp.float32)
    return first, second, rest - second


def six_products(left, right):
    a, b, c = split_three(left)
    p, q, r = split_three(right)
    return (a, a, b, b, a, c), (p, q, p, q, r, p)


def feature_body(n_source, n_target, *refs):
    source_ref, target_ref, rows = refs[n_source + n_target :]
    points = rows.shape[1]
    rows[27:FEATURES, :] = jnp.zeros((FEATURES - 27, points), jnp.float32)
    for i in range(n_source + n_target):
        points_ref = refs[i]
        centred = points_ref[0:3, :points] - 0.5
        square = centred * centred
        norm = square[0:1] + square[1:2] + square[2:3]
        if i < n_source:
            root = 1.0 / (points_ref[3:4, :points] * INV_FOUR_PI)
            scale = root * root
            side, shared, last = 1, (centred * scale, scale), scale * (norm + DELTA_SQ)
            out = source_ref.at[:, i * points : (i + 1) * points]
        else:
            side, shared, last = 0, (-2.0 * centred, norm), None
            out = target_ref.at[:, (i - n_source) * points : (i - n_source + 1) * points]
        first = 0
        for values in shared:
            for part in six_products(values, values)[side]:
                rows[first : first + values.shape[0], :] = part
                first += values.shape[0]
        parts = [jnp.ones_like(norm)] * 3 if last is None else split_three(last)
        for part in parts:
            rows[first : first + 1, :] = part
            first += 1
        out[...] = rows[...].astype(jnp.bfloat16)


def turned_block(source, target):
    scaled = lax.dot_general(
        source, target, (((0,), (0,)), ((), ())), preferred_element_type=jnp.float32
    )
    return lax.rsqrt(scaled).astype(jnp.bfloat16)


def local_body(
    first, offset_ref, near_ref, target_ref, source_ref, probes_ref, out_ref,
    even_ref, odd_ref, omega_ref, sem,
):
    fetch = pltpu.make_async_copy(probes_ref, omega_ref, sem)
    fetch.start()
    entries = near_ref.shape[1]
    leaves = out_ref.shape[1] // LEAF_PTS
    offset = offset_ref[0]

    def source_of(t, e):
        return leaf_range(near_ref[first + t, e] - offset)

    def make(t, block_ref):
        target = target_ref[:, leaf_range(first + t)]
        for e in range(entries):
            block_ref[e * LEAF_PTS : (e + 1) * LEAF_PTS, :] = turned_block(
                source_ref[:, source_of(t, e)], target
            )

    def use(t, block_ref):
        probes = jnp.concatenate([omega_ref[:, source_of(t, e)] for e in range(entries)], axis=1)
        out_ref[:, leaf_range(t)] = jnp.dot(
            probes, block_ref[...], preferred_element_type=jnp.float32
        )

    make(0, even_ref)
    fetch.wait()

    def step(k, carry):
        make(2 * k + 1, odd_ref)
        use(2 * k, even_ref)
        make(jnp.minimum(2 * k + 2, leaves - 1), even_ref)
        use(2 * k + 1, odd_ref)
        return carry

    lax.fori_loop(0, leaves // 2, step, 0)


def far_body(first, count_ref, table_ref, source_ref, target_ref, *refs):
    omegas = refs[:4]
    own_ref, rest_ref, block_ref, total_ref, omega_ref, sems = refs[4:]
    size, points = own_ref.shape
    fetches = []
    for k in range(4):
        rows = pl.ds(first if k < 3 else 0, size)
        fetches.append(
            pltpu.make_async_copy(
                omegas[k].at[rows, :],
                omega_ref.at[:, k * points : (k + 1) * points],
                sems.at[k],
            )
        )
        fetches[-1].start()
    count = count_ref[0]
    total_ref[...] = jnp.zeros_like(total_ref)
    for fetch in fetches:
        fetch.wait()

    def step(k, carry):
        for u in range(BATCH):
            item = k * BATCH + u
            block_ref[u] = turned_block(
                source_ref[:, leaf_range(table_ref[0, item])],
                target_ref[:, leaf_range(table_ref[1, item])],
            )
        for u in range(BATCH):
            item = k * BATCH + u
            product = jnp.dot(
                omega_ref[:, leaf_range(table_ref[0, item])],
                block_ref[u],
                preferred_element_type=jnp.float32,
            )
            total_ref[:, leaf_range(table_ref[1, item])] += jnp.where(item < count, product, 0.0)
        return carry

    lax.fori_loop(0, lax.div(count + BATCH - 1, BATCH), step, 0)
    own_ref[...] = total_ref[:, :points]
    for r in range(1, rest_ref.shape[0] + 1):
        rest_ref[r - 1] = total_ref[:, r * points : (r + 1) * points].astype(jnp.bfloat16)


def pick_body(skel_ref, interp_ref, out_ref):
    turned = jnp.transpose(skel_ref[...].astype(jnp.float32)).astype(jnp.int32)
    lane = lax.broadcasted_iota(jnp.int32, (SK, LEAF_PTS), 1)
    for leaf in range(skel_ref.shape[0]):
        parent, child = divmod(leaf, CHILD)
        chosen = (turned[:, leaf : leaf + 1] == lane).astype(jnp.float32).astype(jnp.bfloat16)
        out_ref[parent, :, child * LEAF_PTS : (child + 1) * LEAF_PTS] = jnp.dot(
            interp_ref[parent, :, child * SK : (child + 1) * SK],
            chosen,
            preferred_element_type=jnp.float32,
        ).astype(jnp.bfloat16)


def merge_body(n_local, n_chunk, *refs):
    locals_ = refs[:n_local]
    owns = refs[n_local : n_local + n_chunk]
    arrived = refs[n_local + n_chunk : n_local + 2 * n_chunk]
    pick_ref, near_ref, merged_ref, energy_ref = refs[n_local + 2 * n_chunk :]
    width = locals_[0].shape[1]
    for i in range(n_local):
        columns = slice(i * width, (i + 1) * width)
        first = 0
        for own_ref, arrived_ref in zip(owns, arrived):
            rows = slice(first, first + own_ref.shape[0])
            first += own_ref.shape[0]
            near_ref[rows, columns] = (
                locals_[i][rows, :]
                + own_ref[:, columns]
                + arrived_ref[:, columns].astype(jnp.float32)
            )
    parents, _, width = pick_ref.shape
    for p in range(parents):
        merged = lax.dot_general(
            near_ref[:, p * width : (p + 1) * width].astype(jnp.bfloat16),
            pick_ref[p],
            (((1,), (1,)), ((), ())),
            preferred_element_type=jnp.float32,
        )
        merged_ref[:, p * SK2 : (p + 1) * SK2] = merged
        energy_ref[p : p + 1, :] = jnp.broadcast_to(
            jnp.sum(jnp.sum(merged * merged, axis=0, keepdims=True), axis=1, keepdims=True),
            (1, LEAF_PTS),
        )


def scale_body(count, merged_ref, *refs):
    energies, out_ref = refs[:-1], refs[-1]
    energy = sum(ref[...] for ref in energies[1:]) + energies[0][...]
    for p in range(energy.shape[0]):
        factor = lax.rsqrt(energy[p : p + 1, 0:SK2] / count + 1e-06)
        out_ref[:, p * SK2 : (p + 1) * SK2] = merged_ref[:, p * SK2 : (p + 1) * SK2] * factor


def call(body, out_shape, in_specs, scratch=(), micros=1.0):
    many = isinstance(out_shape, (tuple, list))
    return pl.pallas_call(
        body,
        out_shape=out_shape,
        in_specs=in_specs,
        out_specs=[VMEM] * len(out_shape) if many else VMEM,
        scratch_shapes=list(scratch),
        compiler_params=pltpu.CompilerParams(vmem_limit_bytes=VMEM_LIMIT),
        cost_estimate=pl.CostEstimate(
            flops=int(micros * 1e7), bytes_accessed=int(micros * 3e4), transcendentals=0
        ),
    )


def features_of(points, sources, targets):
    return call(
        functools.partial(feature_body, len(sources), len(targets)),
        [
            jax.ShapeDtypeStruct((FEATURES, len(sources) * points), jnp.bfloat16),
            jax.ShapeDtypeStruct((FEATURES, len(targets) * points), jnp.bfloat16),
        ],
        [VMEM] * (len(sources) + len(targets)),
        [pltpu.VMEM((FEATURES, points), jnp.float32)],
    )(*sources, *targets)


def exchange(array, axis, bit):
    size = lax.axis_size(axis)
    return lax.ppermute(array, axis, [(i, i ^ bit) for i in range(size)])


def after(array, *others):
    return lax.optimization_barrier((array, *others))[0]


def far_table(pairs, me, masks, outer, leaf_dev, length):
    member = jnp.arange(4, dtype=jnp.int32)
    owners = me ^ (member % 2 * masks[0] + member // 2 * masks[1])
    source = pairs[:, 0] - ((owners - member) * leaf_dev)[:, None]
    relation = (pairs[:, 1] // leaf_dev) ^ me
    inside = ((relation & outer) == 0).reshape(-1)
    target = (relation // 2) * leaf_dev + pairs[:, 1] % leaf_dev
    iota = jnp.arange(inside.shape[0], dtype=jnp.int32)
    place = jnp.sum(
        (inside[:, None] & (iota[:, None] < iota[None, :])).astype(jnp.int32), axis=0
    )
    place = jnp.where(inside, place, -1)
    hit = place[None, None, :] == jnp.arange(length, dtype=jnp.int32)[None, :, None]
    codes = jnp.stack([source.reshape(-1), target.reshape(-1)])
    return (
        jnp.sum(inside.astype(jnp.int32)).reshape(1),
        jnp.sum(jnp.where(hit, codes[:, None, :], 0), axis=2),
    )


def per_device(coords, weights, omega, near_local, far_pairs, skel_rows, parent_interp):
    n_leaf = lax.axis_size("leaf")
    points = coords.shape[1]
    leaf_dev = points // LEAF_PTS
    probe_dev = omega.shape[0]
    parent_dev = leaf_dev // CHILD
    me = lax.axis_index("leaf")
    top, low = n_leaf // 2, 1
    dests = n_leaf // 4
    pair_dev = far_pairs.shape[1]
    unit = probe_dev // sum(CHUNKS)
    chunks = [(unit * sum(CHUNKS[:i]), unit * c) for i, c in enumerate(CHUNKS)]

    omega_across = exchange(omega, "leaf", top)
    pair_columns = 2 * pair_dev // 4
    sent = jnp.concatenate(
        [
            jnp.concatenate([coords, weights[None]], axis=0),
            far_pairs.reshape(4, pair_columns).astype(jnp.float32),
        ],
        axis=1,
    )
    across = exchange(sent, "leaf", top)
    both = exchange(sent, "leaf", top | low)

    source, target = features_of(points, [sent], [sent])
    part_points = points // LOCAL_PARTS
    entries = near_local.shape[1]

    def local_part(i, table):
        return call(
            functools.partial(local_body, i * part_points // LEAF_PTS),
            jax.ShapeDtypeStruct((probe_dev, part_points), jnp.float32),
            [SMEM, SMEM, VMEM, VMEM, HBM],
            [pltpu.VMEM((entries * LEAF_PTS, LEAF_PTS), jnp.bfloat16)] * 2
            + [pltpu.VMEM((probe_dev, points), jnp.bfloat16), pltpu.SemaphoreType.DMA],
            micros=16.0 / LOCAL_PARTS,
        )((me * leaf_dev).reshape(1), table, target, source, omega)

    omega_beside = exchange(omega, "leaf", low)
    local = [local_part(i, near_local) for i in range(LOCAL_PARTS)]
    omega_across = after(omega_across, omega_beside, *local)
    late = after(sent, omega_across)
    beside = exchange(late, "leaf", low)
    partners = [exchange(late, "leaf", 2 * r) for r in range(1, dests)]
    relayed = []
    for first, size in chunks:
        part = omega_across[first : first + size]
        if relayed:
            part = after(omega_across, relayed[-1])[first : first + size]
        relayed.append(exchange(part, "leaf", low))

    bundles = [sent, across, beside, both]
    bundles = list(lax.optimization_barrier((*bundles, relayed[0]))[:-1])
    pairs = jnp.stack([b[:, points:].astype(jnp.int32).reshape(2, pair_dev) for b in bundles])
    slots = (dests * 4 * CAP + BATCH - 1) // BATCH * BATCH
    far_count, codes = far_table(
        pairs, me, (top, low), top | low, leaf_dev, slots
    )
    far_source, far_target = features_of(points, bundles, [bundles[0], *partners])
    owns, arrived = [], []
    for (first, size), omega_both in zip(chunks, relayed):
        own, rest = call(
            functools.partial(far_body, first),
            [
                jax.ShapeDtypeStruct((size, points), jnp.float32),
                jax.ShapeDtypeStruct((dests - 1, size, points), jnp.bfloat16),
            ],
            [SMEM, SMEM, VMEM, VMEM] + [HBM] * 4,
            [
                pltpu.VMEM((BATCH, LEAF_PTS, LEAF_PTS), jnp.bfloat16),
                pltpu.VMEM((size, dests * points), jnp.float32),
                pltpu.VMEM((size, 4 * points), jnp.bfloat16),
                pltpu.SemaphoreType.DMA((4,)),
            ],
            micros=4.0,
        )(
            far_count, codes, far_source, far_target, omega, omega_across, omega_beside, omega_both
        )
        half = dests // 2
        while half > 1:
            got = exchange(rest[half - 1 :], "leaf", 2 * half)
            own = own + got[0].astype(jnp.float32)
            rest = rest[: half - 1] + got[1:]
            half //= 2
        owns.append(own)
        arrived.append(exchange(rest[0], "leaf", 2))
    pick = call(
        pick_body,
        jax.ShapeDtypeStruct((parent_dev, SK2, CHILD * LEAF_PTS), jnp.bfloat16),
        [VMEM] * 2,
    )(skel_rows, parent_interp.transpose(0, 2, 1))
    near, merged, energy = call(
        functools.partial(merge_body, LOCAL_PARTS, len(chunks)),
        [
            jax.ShapeDtypeStruct((probe_dev, points), jnp.float32),
            jax.ShapeDtypeStruct((probe_dev, parent_dev * SK2), jnp.float32),
            jax.ShapeDtypeStruct((parent_dev, LEAF_PTS), jnp.float32),
        ],
        [VMEM] * (LOCAL_PARTS + 2 * len(chunks) + 1),
        micros=2.0,
    )(*local, *owns, *arrived, pick)
    n_probe = lax.axis_size("probe")
    if n_probe & (n_probe - 1):
        energies = [lax.psum(energy, "probe")]
    else:
        energies = [energy] + [exchange(energy, "probe", k) for k in range(1, n_probe)]
    parent = call(
        functools.partial(scale_body, float(SK2 * probe_dev * n_probe)),
        jax.ShapeDtypeStruct((probe_dev, parent_dev * SK2), jnp.float32),
        [VMEM] * (1 + len(energies)),
    )(merged, *energies)
    return near, parent


def solution(mesh):
    return jax.shard_map(
        per_device,
        mesh=mesh,
        in_specs=(
            P(None, "leaf"),
            P("leaf"),
            P("probe", "leaf"),
            P("leaf", None),
            P(None, "leaf"),
            P("leaf", None),
            P("leaf", None, None),
        ),
        out_specs=(P("probe", "leaf"), P("probe", "leaf")),
        check_vma=False,
    )
```

```python
import functools

import jax
import jax.numpy as jnp
from jax import lax
from jax.experimental import pallas as pl
from jax.experimental.pallas import tpu as pltpu
from jax.sharding import PartitionSpec as P

LEAF_PTS = 128
SK = 32
SK2 = 64
CHILD = 8
CAP = 16

DELTA_SQ = 0.0001
INV_FOUR_PI = 0.07957747154594767

VMEM_LIMIT = 12 * 1024 * 1024
BATCH = 24
FEATURES = 32
CHUNKS = (1, 1)
LOCAL_PARTS = 1

SMEM = pl.BlockSpec(memory_space=pltpu.SMEM)
VMEM = pl.BlockSpec(memory_space=pltpu.VMEM)
HBM = pl.BlockSpec(memory_space=pltpu.HBM)


def leaf_range(leaf):
    return pl.ds(pl.multiple_of(leaf * LEAF_PTS, LEAF_PTS), LEAF_PTS)


def split_three(values):
    first = values.astype(jnp.bfloat16).astype(jnp.float32)
    rest = values - first
    second = rest.astype(jnp.bfloat16).astype(jnp.float32)
    return first, second, rest - second


def six_products(left, right):
    a, b, c = split_three(left)
    p, q, r = split_three(right)
    return (a, a, b, b, a, c), (p, q, p, q, r, p)


def write_features(points_ref, rows, out, is_source):
    points = rows.shape[1]
    centred = points_ref[0:3, :points] - 0.5
    square = centred * centred
    norm = square[0:1] + square[1:2] + square[2:3]
    if is_source:
        root = 1.0 / (points_ref[3:4, :points] * INV_FOUR_PI)
        scale = root * root
        side, shared, last = 1, (centred * scale, scale), scale * (norm + DELTA_SQ)
    else:
        side, shared, last = 0, (-2.0 * centred, norm), None
    first = 0
    for values in shared:
        for part in six_products(values, values)[side]:
            rows[first : first + values.shape[0], :] = part
            first += values.shape[0]
    parts = [jnp.ones_like(norm)] * 3 if last is None else split_three(last)
    for part in parts:
        rows[first : first + 1, :] = part
        first += 1
    out[...] = rows[...].astype(jnp.bfloat16)


def feature_body(n_bundle, place_ref, *refs):
    source_ref, target_ref, rows = refs[-3:]
    points = rows.shape[1]
    if len(refs) > n_bundle + 3:
        own_source_ref, own_target_ref = refs[n_bundle:-3]
        source_ref[:, :points] = own_source_ref[...]
        target_ref[:, :points] = own_target_ref[:, :points]
    target_ref[:, target_ref.shape[1] - LEAF_PTS :] = jnp.ones((FEATURES, LEAF_PTS), jnp.bfloat16)
    rows[27:FEATURES, :] = jnp.zeros((FEATURES - 27, points), jnp.float32)
    for i in range(n_bundle):
        for kind, out_ref in enumerate((source_ref, target_ref)):
            place = place_ref[kind, i]

            @pl.when(place >= 0)
            def _(points_ref=refs[i], place=place, out_ref=out_ref, kind=kind):
                lanes = pl.ds(pl.multiple_of(place * points, LEAF_PTS), points)
                write_features(points_ref, rows, out_ref.at[:, lanes], kind == 0)


def turned_block(source, target):
    scaled = lax.dot_general(
        source, target, (((0,), (0,)), ((), ())), preferred_element_type=jnp.float32
    )
    return lax.rsqrt(scaled).astype(jnp.bfloat16)


def local_body(
    first, offset_ref, near_ref, target_ref, source_ref, probes_ref, out_ref,
    even_ref, odd_ref, omega_ref, sem,
):
    fetch = pltpu.make_async_copy(probes_ref, omega_ref, sem)
    fetch.start()
    entries = near_ref.shape[1]
    leaves = out_ref.shape[1] // LEAF_PTS
    offset = offset_ref[0]

    def source_of(t, e):
        return leaf_range(near_ref[first + t, e] - offset)

    def make(t, block_ref):
        target = target_ref[:, leaf_range(first + t)]
        for e in range(entries):
            block_ref[e * LEAF_PTS : (e + 1) * LEAF_PTS, :] = turned_block(
                source_ref[:, source_of(t, e)], target
            )

    def use(t, block_ref):
        probes = jnp.concatenate([omega_ref[:, source_of(t, e)] for e in range(entries)], axis=1)
        out_ref[:, leaf_range(t)] = jnp.dot(
            probes, block_ref[...], preferred_element_type=jnp.float32
        )

    make(0, even_ref)
    fetch.wait()

    def step(k, carry):
        make(2 * k + 1, odd_ref)
        use(2 * k, even_ref)
        make(jnp.minimum(2 * k + 2, leaves - 1), even_ref)
        use(2 * k + 1, odd_ref)
        return carry

    lax.fori_loop(0, leaves // 2, step, 0)


def far_body(first, table_ref, source_ref, target_ref, *refs):
    omegas = refs[:4]
    own_ref, rest_ref, block_ref, total_ref, omega_ref, sems = refs[4:]
    size, points = own_ref.shape
    fetches = []
    for k, slot in enumerate((0, 2, 1, 3)):
        rows = pl.ds(first if k < 2 else 0, size)
        fetches.append(
            pltpu.make_async_copy(
                omegas[k].at[rows, :],
                omega_ref.at[:, slot * points : (slot + 1) * points],
                sems.at[k],
            )
        )
        fetches[-1].start()
    total_ref[...] = jnp.zeros_like(total_ref)
    spare = total_ref.shape[1] // LEAF_PTS - 1
    rounds = sum(
        (table_ref[1, k] < spare).astype(jnp.int32) for k in range(0, table_ref.shape[1], BATCH)
    )
    for fetch in fetches:
        fetch.wait()

    def step(k, carry):
        for u in range(BATCH):
            item = k * BATCH + u
            block_ref[u] = turned_block(
                source_ref[:, leaf_range(table_ref[0, item])],
                target_ref[:, leaf_range(table_ref[1, item])],
            )
        for u in range(BATCH):
            item = k * BATCH + u
            product = jnp.dot(
                omega_ref[:, leaf_range(table_ref[0, item])],
                block_ref[u],
                preferred_element_type=jnp.float32,
            )
            total_ref[:, leaf_range(table_ref[1, item])] += product
        return carry

    lax.fori_loop(0, rounds, step, 0)
    own_ref[...] = total_ref[:, :points]
    for r in range(1, rest_ref.shape[0] + 1):
        rest_ref[r - 1] = total_ref[:, r * points : (r + 1) * points].astype(jnp.bfloat16)


def pick_body(skel_ref, interp_ref, out_ref):
    turned = jnp.transpose(skel_ref[...].astype(jnp.float32)).astype(jnp.int32)
    lane = lax.broadcasted_iota(jnp.int32, (SK, LEAF_PTS), 1)
    for leaf in range(skel_ref.shape[0]):
        parent, child = divmod(leaf, CHILD)
        chosen = (turned[:, leaf : leaf + 1] == lane).astype(jnp.float32).astype(jnp.bfloat16)
        out_ref[parent, :, child * LEAF_PTS : (child + 1) * LEAF_PTS] = jnp.dot(
            interp_ref[parent, :, child * SK : (child + 1) * SK],
            chosen,
            preferred_element_type=jnp.float32,
        ).astype(jnp.bfloat16)


def merge_body(n_local, n_chunk, *refs):
    locals_ = refs[:n_local]
    owns = refs[n_local : n_local + n_chunk]
    arrived = refs[n_local + n_chunk : n_local + 2 * n_chunk]
    pick_ref, near_ref, merged_ref, energy_ref = refs[n_local + 2 * n_chunk :]
    width = locals_[0].shape[1]
    for i in range(n_local):
        columns = slice(i * width, (i + 1) * width)
        first = 0
        for own_ref, arrived_ref in zip(owns, arrived):
            rows = slice(first, first + own_ref.shape[0])
            first += own_ref.shape[0]
            near_ref[rows, columns] = (
                locals_[i][rows, :]
                + own_ref[:, columns]
                + arrived_ref[:, columns].astype(jnp.float32)
            )
    parents, _, width = pick_ref.shape
    for p in range(parents):
        merged = lax.dot_general(
            near_ref[:, p * width : (p + 1) * width].astype(jnp.bfloat16),
            pick_ref[p],
            (((1,), (1,)), ((), ())),
            preferred_element_type=jnp.float32,
        )
        merged_ref[:, p * SK2 : (p + 1) * SK2] = merged
        energy_ref[p : p + 1, :] = jnp.broadcast_to(
            jnp.sum(jnp.sum(merged * merged, axis=0, keepdims=True), axis=1, keepdims=True),
            (1, LEAF_PTS),
        )


def scale_body(count, merged_ref, *refs):
    energies, out_ref = refs[:-1], refs[-1]
    energy = sum(ref[...] for ref in energies[1:]) + energies[0][...]
    for p in range(energy.shape[0]):
        factor = lax.rsqrt(energy[p : p + 1, 0:SK2] / count + 1e-06)
        out_ref[:, p * SK2 : (p + 1) * SK2] = merged_ref[:, p * SK2 : (p + 1) * SK2] * factor


def call(body, out_shape, in_specs, scratch=(), micros=1.0):
    many = isinstance(out_shape, (tuple, list))
    return pl.pallas_call(
        body,
        out_shape=out_shape,
        in_specs=in_specs,
        out_specs=[VMEM] * len(out_shape) if many else VMEM,
        scratch_shapes=list(scratch),
        compiler_params=pltpu.CompilerParams(vmem_limit_bytes=VMEM_LIMIT),
        cost_estimate=pl.CostEstimate(
            flops=int(micros * 1e7), bytes_accessed=int(micros * 3e4), transcendentals=0
        ),
    )


def features_of(points, senders, dests, places, bundles, own=()):
    return call(
        functools.partial(feature_body, len(bundles)),
        [
            jax.ShapeDtypeStruct((FEATURES, senders * points), jnp.bfloat16),
            jax.ShapeDtypeStruct((FEATURES, dests * points + LEAF_PTS), jnp.bfloat16),
        ],
        [SMEM] + [VMEM] * (len(bundles) + len(own)),
        [pltpu.VMEM((FEATURES, points), jnp.float32)],
    )(places, *bundles, *own)


def exchange(array, axis, bit):
    size = lax.axis_size(axis)
    return lax.ppermute(array, axis, [(i, i ^ bit) for i in range(size)])


def after(array, *others):
    return lax.optimization_barrier((array, *others))[0]


def gather_bundles(sent, top, low, dests, wait):
    masks = [top, low, top | low] + [2 * r for r in range(1, dests)]
    n_leaf, n_probe = lax.axis_size("leaf"), lax.axis_size("probe")
    if len(masks) != 4 or n_probe % 2:
        rank = jnp.arange(len(masks), dtype=jnp.int32)
        bundles = [exchange(sent, "leaf", mask) for mask in masks]
    else:
        core = lax.axis_index("probe") % 2
        rank = jnp.stack([core, 2 + core, 1 - core, 3 - core])
        bundles = []
        for half in (0, 2):
            pairs = [
                (i * n_probe + q, (i ^ masks[half + q % 2]) * n_probe + q)
                for i in range(n_leaf)
                for q in range(n_probe)
            ]
            bundles.append(lax.ppermute(sent, ("leaf", "probe"), pairs))
        bundles = list(lax.optimization_barrier((*bundles, *wait))[:2])
        bundles += [exchange(bundle, "probe", 1) for bundle in bundles]
    distance = jnp.where(
        rank < 3, (rank + 1) % 2 * top + (rank + 1) // 2 % 2 * low, 2 * (rank - 2)
    )
    distance = jnp.where(rank == 2, top | low, distance)
    sender = jnp.where(rank < 3, rank + 1, -1)
    member = jnp.where(rank < 3, -1, rank - 2)
    zero = jnp.zeros((1,), jnp.int32)
    return (
        [sent, *bundles],
        jnp.concatenate([zero, distance]),
        jnp.stack([jnp.concatenate([zero, sender]), jnp.concatenate([zero, member])]),
    )


def far_table(pairs, me, distance, sender, outer, leaf_dev, length, spare):
    source = pairs[:, 0] - (((me ^ distance) - sender) * leaf_dev)[:, None]
    relation = (pairs[:, 1] // leaf_dev) ^ me
    inside = (((relation & outer) == 0) & (sender >= 0)[:, None]).reshape(-1)
    target = (relation // 2) * leaf_dev + pairs[:, 1] % leaf_dev
    iota = jnp.arange(inside.shape[0], dtype=jnp.int32)
    place = jnp.sum(
        (inside[:, None] & (iota[:, None] < iota[None, :])).astype(jnp.int32), axis=0
    )
    place = jnp.where(inside, place, -1)
    hit = place[None, None, :] == jnp.arange(length, dtype=jnp.int32)[None, :, None]
    codes = jnp.stack([source.reshape(-1), target.reshape(-1) - spare])
    return jnp.sum(jnp.where(hit, codes[:, None, :], 0), axis=2) + jnp.array([[0], [spare]])


def per_device(coords, weights, omega, near_local, far_pairs, skel_rows, parent_interp):
    n_leaf = lax.axis_size("leaf")
    points = coords.shape[1]
    leaf_dev = points // LEAF_PTS
    probe_dev = omega.shape[0]
    parent_dev = leaf_dev // CHILD
    me = lax.axis_index("leaf")
    top, low = n_leaf // 2, 1
    dests = n_leaf // 4
    pair_dev = far_pairs.shape[1]
    unit = probe_dev // sum(CHUNKS)
    chunks = [(unit * sum(CHUNKS[:i]), unit * c) for i, c in enumerate(CHUNKS)]

    parts = lax.optimization_barrier([omega[first : first + size] for first, size in chunks])
    crossed = [exchange(part, "leaf", top) for part in parts]
    omega_beside = exchange(after(omega, *parts), "leaf", low)
    pair_columns = 2 * pair_dev // 4
    sent = jnp.concatenate(
        [
            jnp.concatenate([coords, weights[None]], axis=0),
            far_pairs.reshape(4, pair_columns).astype(jnp.float32),
        ],
        axis=1,
    )
    source, target = features_of(points, 1, 1, jnp.zeros((2, 1), jnp.int32), [sent])
    part_points = points // LOCAL_PARTS
    entries = near_local.shape[1]

    def local_part(i, table):
        return call(
            functools.partial(local_body, i * part_points // LEAF_PTS),
            jax.ShapeDtypeStruct((probe_dev, part_points), jnp.float32),
            [SMEM, SMEM, VMEM, VMEM, HBM],
            [pltpu.VMEM((entries * LEAF_PTS, LEAF_PTS), jnp.bfloat16)] * 2
            + [pltpu.VMEM((probe_dev, points), jnp.bfloat16), pltpu.SemaphoreType.DMA],
            micros=16.0 / LOCAL_PARTS,
        )((me * leaf_dev).reshape(1), table, target, source, omega)

    local = [local_part(i, near_local) for i in range(LOCAL_PARTS)]
    bundles, distance, places = gather_bundles(sent, top, low, dests, [crossed[0], *local])
    relayed = []
    for i, part in enumerate(crossed):
        crossed[i] = after(part, relayed[-1]) if relayed else after(part, omega_beside, *local)
        relayed.append(exchange(crossed[i], "leaf", low))

    bundles = list(lax.optimization_barrier((*bundles, relayed[0]))[:-1])
    pairs = jnp.stack([b[:, points:].astype(jnp.int32).reshape(2, pair_dev) for b in bundles])
    slots = (dests * 4 * CAP + BATCH - 1) // BATCH * BATCH
    codes = far_table(
        pairs, me, distance, places[0], top | low, leaf_dev, slots, dests * leaf_dev
    )
    far_source, far_target = features_of(
        points, 4, dests, places, bundles
    )
    owns, arrived = [], []
    for (first, size), from_across, from_both in zip(chunks, crossed, relayed):
        own, rest = call(
            functools.partial(far_body, first),
            [
                jax.ShapeDtypeStruct((size, points), jnp.float32),
                jax.ShapeDtypeStruct((dests - 1, size, points), jnp.bfloat16),
            ],
            [SMEM, VMEM, VMEM] + [HBM] * 4,
            [
                pltpu.VMEM((BATCH, LEAF_PTS, LEAF_PTS), jnp.bfloat16),
                pltpu.VMEM((size, dests * points + LEAF_PTS), jnp.float32),
                pltpu.VMEM((size, 4 * points), jnp.bfloat16),
                pltpu.SemaphoreType.DMA((4,)),
            ],
            micros=4.0,
        )(
            codes, far_source, far_target, omega, omega_beside, from_across, from_both
        )
        half = dests // 2
        while half > 1:
            got = exchange(rest[half - 1 :], "leaf", 2 * half)
            own = own + got[0].astype(jnp.float32)
            rest = rest[: half - 1] + got[1:]
            half //= 2
        owns.append(own)
        arrived.append(exchange(rest[0], "leaf", 2))
    pick = call(
        pick_body,
        jax.ShapeDtypeStruct((parent_dev, SK2, CHILD * LEAF_PTS), jnp.bfloat16),
        [VMEM] * 2,
    )(skel_rows, parent_interp.transpose(0, 2, 1))
    near, merged, energy = call(
        functools.partial(merge_body, LOCAL_PARTS, len(chunks)),
        [
            jax.ShapeDtypeStruct((probe_dev, points), jnp.float32),
            jax.ShapeDtypeStruct((probe_dev, parent_dev * SK2), jnp.float32),
            jax.ShapeDtypeStruct((parent_dev, LEAF_PTS), jnp.float32),
        ],
        [VMEM] * (LOCAL_PARTS + 2 * len(chunks) + 1),
        micros=2.0,
    )(*local, *owns, *arrived, pick)
    n_probe = lax.axis_size("probe")
    if n_probe & (n_probe - 1):
        energies = [lax.psum(energy, "probe")]
    else:
        energies = [energy] + [exchange(energy, "probe", k) for k in range(1, n_probe)]
    parent = call(
        functools.partial(scale_body, float(SK2 * probe_dev * n_probe)),
        jax.ShapeDtypeStruct((probe_dev, parent_dev * SK2), jnp.float32),
        [VMEM] * (1 + len(energies)),
    )(merged, *energies)
    return near, parent


def solution(mesh):
    return jax.shard_map(
        per_device,
        mesh=mesh,
        in_specs=(
            P(None, "leaf"),
            P("leaf"),
            P("probe", "leaf"),
            P("leaf", None),
            P(None, "leaf"),
            P("leaf", None),
            P("leaf", None, None),
        ),
        out_specs=(P("probe", "leaf"), P("probe", "leaf")),
        check_vma=False,
    )
```

```python
import functools

import jax
import jax.numpy as jnp
from jax import lax
from jax.experimental import pallas as pl
from jax.experimental.pallas import tpu as pltpu
from jax.sharding import PartitionSpec as P

LEAF_PTS = 128
SK = 32
SK2 = 64
CHILD = 8
CAP = 16

DELTA_SQ = 0.0001
INV_FOUR_PI = 0.07957747154594767

VMEM_LIMIT = 12 * 1024 * 1024
BATCH = 24
FEATURES = 32
CHUNKS = (1, 1)
SHARE = 2

SMEM = pl.BlockSpec(memory_space=pltpu.SMEM)
VMEM = pl.BlockSpec(memory_space=pltpu.VMEM)
HBM = pl.BlockSpec(memory_space=pltpu.HBM)


def leaf_range(leaf):
    return pl.ds(pl.multiple_of(leaf * LEAF_PTS, LEAF_PTS), LEAF_PTS)


def split_three(values):
    first = values.astype(jnp.bfloat16).astype(jnp.float32)
    rest = values - first
    second = rest.astype(jnp.bfloat16).astype(jnp.float32)
    return first, second, rest - second


def six_products(left, right):
    a, b, c = split_three(left)
    p, q, r = split_three(right)
    return (a, a, b, b, a, c), (p, q, p, q, r, p)


def write_features(points_ref, rows, out, is_source):
    points = rows.shape[1]
    centred = points_ref[0:3, :points] - 0.5
    square = centred * centred
    norm = square[0:1] + square[1:2] + square[2:3]
    if is_source:
        root = 1.0 / (points_ref[3:4, :points] * INV_FOUR_PI)
        scale = root * root
        side, shared, last = 1, (centred * scale, scale), scale * (norm + DELTA_SQ)
    else:
        side, shared, last = 0, (-2.0 * centred, norm), None
    first = 0
    for values in shared:
        for part in six_products(values, values)[side]:
            rows[first : first + values.shape[0], :] = part
            first += values.shape[0]
    parts = [jnp.ones_like(norm)] * 3 if last is None else split_three(last)
    for part in parts:
        rows[first : first + 1, :] = part
        first += 1
    out[...] = rows[...].astype(jnp.bfloat16)


def feature_body(n_bundle, place_ref, *refs):
    source_ref, target_ref, rows = refs[-3:]
    points = rows.shape[1]
    if len(refs) > n_bundle + 3:
        own_source_ref, own_target_ref = refs[n_bundle:-3]
        source_ref[:, :points] = own_source_ref[...]
        target_ref[:, :points] = own_target_ref[:, :points]
    target_ref[:, target_ref.shape[1] - LEAF_PTS :] = jnp.ones((FEATURES, LEAF_PTS), jnp.bfloat16)
    rows[27:FEATURES, :] = jnp.zeros((FEATURES - 27, points), jnp.float32)
    for i in range(n_bundle):
        for kind, out_ref in enumerate((source_ref, target_ref)):
            place = place_ref[kind, i]

            @pl.when(place >= 0)
            def _(points_ref=refs[i], place=place, out_ref=out_ref, kind=kind):
                lanes = pl.ds(pl.multiple_of(place * points, LEAF_PTS), points)
                write_features(points_ref, rows, out_ref.at[:, lanes], kind == 0)


def turned_block(source, target):
    scaled = lax.dot_general(
        source, target, (((0,), (0,)), ((), ())), preferred_element_type=jnp.float32
    )
    return lax.rsqrt(scaled).astype(jnp.bfloat16)


def local_body(
    place_ref, near_ref, target_ref, source_ref, own_probes_ref, other_probes_ref,
    own_ref, other_ref, even_ref, odd_ref, omega_ref, sems,
):
    probe_dev = own_ref.shape[0]
    fetches = [
        pltpu.make_async_copy(
            ref, omega_ref.at[i * probe_dev : (i + 1) * probe_dev, :], sems.at[i]
        )
        for i, ref in enumerate((own_probes_ref, other_probes_ref))
    ]
    for fetch in fetches:
        fetch.start()
    entries = near_ref.shape[1]
    leaves = own_ref.shape[1] // LEAF_PTS
    offset, first = place_ref[0], place_ref[1]

    def source_of(t, e):
        return leaf_range(near_ref[first + t, e] - offset)

    def make(t, block_ref):
        target = target_ref[:, leaf_range(first + t)]
        for e in range(entries):
            block_ref[e * LEAF_PTS : (e + 1) * LEAF_PTS, :] = turned_block(
                source_ref[:, source_of(t, e)], target
            )

    def use(t, block_ref):
        probes = jnp.concatenate([omega_ref[:, source_of(t, e)] for e in range(entries)], axis=1)
        total = jnp.dot(probes, block_ref[...], preferred_element_type=jnp.float32)
        own_ref[:, leaf_range(t)] = total[:probe_dev]
        other_ref[:, leaf_range(t)] = total[probe_dev:]

    make(0, even_ref)
    for fetch in fetches:
        fetch.wait()

    def step(k, carry):
        make(2 * k + 1, odd_ref)
        use(2 * k, even_ref)
        make(jnp.minimum(2 * k + 2, leaves - 1), even_ref)
        use(2 * k + 1, odd_ref)
        return carry

    lax.fori_loop(0, leaves // 2, step, 0)


def far_body(first, table_ref, source_ref, target_ref, *refs):
    omegas = refs[:4]
    own_ref, rest_ref, block_ref, total_ref, omega_ref, sems = refs[4:]
    size, points = own_ref.shape
    fetches = []
    for k, slot in enumerate((0, 2, 1, 3)):
        rows = pl.ds(first if k < 2 else 0, size)
        fetches.append(
            pltpu.make_async_copy(
                omegas[k].at[rows, :],
                omega_ref.at[:, slot * points : (slot + 1) * points],
                sems.at[k],
            )
        )
        fetches[-1].start()
    total_ref[...] = jnp.zeros_like(total_ref)
    spare = total_ref.shape[1] // LEAF_PTS - 1
    rounds = sum(
        (table_ref[1, k] < spare).astype(jnp.int32) for k in range(0, table_ref.shape[1], BATCH)
    )
    for fetch in fetches:
        fetch.wait()

    def step(k, carry):
        for u in range(BATCH):
            item = k * BATCH + u
            block_ref[u] = turned_block(
                source_ref[:, leaf_range(table_ref[0, item])],
                target_ref[:, leaf_range(table_ref[1, item])],
            )
        for u in range(BATCH):
            item = k * BATCH + u
            product = jnp.dot(
                omega_ref[:, leaf_range(table_ref[0, item])],
                block_ref[u],
                preferred_element_type=jnp.float32,
            )
            total_ref[:, leaf_range(table_ref[1, item])] += product
        return carry

    lax.fori_loop(0, rounds, step, 0)
    own_ref[...] = total_ref[:, :points]
    for r in range(1, rest_ref.shape[0] + 1):
        rest_ref[r - 1] = total_ref[:, r * points : (r + 1) * points].astype(jnp.bfloat16)


def pick_body(skel_ref, interp_ref, out_ref):
    turned = jnp.transpose(skel_ref[...].astype(jnp.float32)).astype(jnp.int32)
    lane = lax.broadcasted_iota(jnp.int32, (SK, LEAF_PTS), 1)
    for leaf in range(skel_ref.shape[0]):
        parent, child = divmod(leaf, CHILD)
        chosen = (turned[:, leaf : leaf + 1] == lane).astype(jnp.float32).astype(jnp.bfloat16)
        out_ref[parent, :, child * LEAF_PTS : (child + 1) * LEAF_PTS] = jnp.dot(
            interp_ref[parent, :, child * SK : (child + 1) * SK],
            chosen,
            preferred_element_type=jnp.float32,
        ).astype(jnp.bfloat16)


def merge_body(n_chunk, side_ref, mine_ref, theirs_ref, *refs):
    owns, arrived = refs[:n_chunk], refs[n_chunk : 2 * n_chunk]
    pick_ref, near_ref, merged_ref, energy_ref = refs[2 * n_chunk :]
    width = mine_ref.shape[1]
    for half in range(SHARE):
        columns = slice(half * width, (half + 1) * width)
        first = 0
        for own_ref, arrived_ref in zip(owns, arrived):
            rows = slice(first, first + own_ref.shape[0])
            first += own_ref.shape[0]
            local = jnp.where(side_ref[0] == half, mine_ref[rows, :], theirs_ref[rows, :])
            near_ref[rows, columns] = (
                local + own_ref[:, columns] + arrived_ref[:, columns].astype(jnp.float32)
            )
    parents, _, width = pick_ref.shape
    for p in range(parents):
        merged = lax.dot_general(
            near_ref[:, p * width : (p + 1) * width].astype(jnp.bfloat16),
            pick_ref[p],
            (((1,), (1,)), ((), ())),
            preferred_element_type=jnp.float32,
        )
        merged_ref[:, p * SK2 : (p + 1) * SK2] = merged
        energy_ref[p : p + 1, :] = jnp.broadcast_to(
            jnp.sum(jnp.sum(merged * merged, axis=0, keepdims=True), axis=1, keepdims=True),
            (1, LEAF_PTS),
        )


def scale_body(count, merged_ref, *refs):
    energies, out_ref = refs[:-1], refs[-1]
    energy = sum(ref[...] for ref in energies[1:]) + energies[0][...]
    for p in range(energy.shape[0]):
        factor = lax.rsqrt(energy[p : p + 1, 0:SK2] / count + 1e-06)
        out_ref[:, p * SK2 : (p + 1) * SK2] = merged_ref[:, p * SK2 : (p + 1) * SK2] * factor


def call(body, out_shape, in_specs, scratch=(), micros=1.0):
    many = isinstance(out_shape, (tuple, list))
    return pl.pallas_call(
        body,
        out_shape=out_shape,
        in_specs=in_specs,
        out_specs=[VMEM] * len(out_shape) if many else VMEM,
        scratch_shapes=list(scratch),
        compiler_params=pltpu.CompilerParams(vmem_limit_bytes=VMEM_LIMIT),
        cost_estimate=pl.CostEstimate(
            flops=int(micros * 1e7), bytes_accessed=int(micros * 3e4), transcendentals=0
        ),
    )


def features_of(points, senders, dests, places, bundles, own=()):
    return call(
        functools.partial(feature_body, len(bundles)),
        [
            jax.ShapeDtypeStruct((FEATURES, senders * points), jnp.bfloat16),
            jax.ShapeDtypeStruct((FEATURES, dests * points + LEAF_PTS), jnp.bfloat16),
        ],
        [SMEM] + [VMEM] * (len(bundles) + len(own)),
        [pltpu.VMEM((FEATURES, points), jnp.float32)],
    )(places, *bundles, *own)


def exchange(array, axis, bit):
    size = lax.axis_size(axis)
    return lax.ppermute(array, axis, [(i, i ^ bit) for i in range(size)])


def after(array, *others):
    return lax.optimization_barrier((array, *others))[0]


def gather_bundles(sent, top, low, dests, wait):
    masks = [top, low, top | low] + [2 * r for r in range(1, dests)]
    n_leaf, n_probe = lax.axis_size("leaf"), lax.axis_size("probe")
    if len(masks) != 4 or n_probe % 2:
        rank = jnp.arange(len(masks), dtype=jnp.int32)
        bundles = [exchange(sent, "leaf", mask) for mask in masks]
    else:
        core = lax.axis_index("probe") % 2
        rank = jnp.stack([core, 2 + core, 1 - core, 3 - core])
        bundles = []
        for half in (0, 2):
            pairs = [
                (i * n_probe + q, (i ^ masks[half + q % 2]) * n_probe + q)
                for i in range(n_leaf)
                for q in range(n_probe)
            ]
            bundles.append(lax.ppermute(sent, ("leaf", "probe"), pairs))
        bundles = list(lax.optimization_barrier((*bundles, *wait))[:2])
        bundles += [exchange(bundle, "probe", 1) for bundle in bundles]
    distance = jnp.where(
        rank < 3, (rank + 1) % 2 * top + (rank + 1) // 2 % 2 * low, 2 * (rank - 2)
    )
    distance = jnp.where(rank == 2, top | low, distance)
    sender = jnp.where(rank < 3, rank + 1, -1)
    member = jnp.where(rank < 3, -1, rank - 2)
    zero = jnp.zeros((1,), jnp.int32)
    return (
        [sent, *bundles],
        jnp.concatenate([zero, distance]),
        jnp.stack([jnp.concatenate([zero, sender]), jnp.concatenate([zero, member])]),
    )


def far_table(pairs, me, distance, sender, outer, leaf_dev, length, spare):
    source = pairs[:, 0] - (((me ^ distance) - sender) * leaf_dev)[:, None]
    relation = (pairs[:, 1] // leaf_dev) ^ me
    inside = (((relation & outer) == 0) & (sender >= 0)[:, None]).reshape(-1)
    target = (relation // 2) * leaf_dev + pairs[:, 1] % leaf_dev
    iota = jnp.arange(inside.shape[0], dtype=jnp.int32)
    place = jnp.sum(
        (inside[:, None] & (iota[:, None] < iota[None, :])).astype(jnp.int32), axis=0
    )
    place = jnp.where(inside, place, -1)
    hit = place[None, None, :] == jnp.arange(length, dtype=jnp.int32)[None, :, None]
    codes = jnp.stack([source.reshape(-1), target.reshape(-1) - spare])
    return jnp.sum(jnp.where(hit, codes[:, None, :], 0), axis=2) + jnp.array([[0], [spare]])


def per_device(coords, weights, omega, near_local, far_pairs, skel_rows, parent_interp):
    n_leaf = lax.axis_size("leaf")
    points = coords.shape[1]
    leaf_dev = points // LEAF_PTS
    probe_dev = omega.shape[0]
    parent_dev = leaf_dev // CHILD
    me = lax.axis_index("leaf")
    top, low = n_leaf // 2, 1
    dests = n_leaf // 4
    pair_dev = far_pairs.shape[1]
    unit = probe_dev // sum(CHUNKS)
    chunks = [(unit * sum(CHUNKS[:i]), unit * c) for i, c in enumerate(CHUNKS)]

    omega_other = exchange(omega, "probe", 1)
    parts = lax.optimization_barrier([omega[first : first + size] for first, size in chunks])
    crossed = [exchange(part, "leaf", top) for part in parts]
    coords = after(coords, *parts)
    omega_beside = exchange(after(omega, *parts), "leaf", low)
    pair_columns = 2 * pair_dev // 4
    sent = jnp.concatenate(
        [
            jnp.concatenate([coords, weights[None]], axis=0),
            far_pairs.reshape(4, pair_columns).astype(jnp.float32),
        ],
        axis=1,
    )
    source, target = features_of(points, 1, 1, jnp.zeros((2, 1), jnp.int32), [sent])
    side = (lax.axis_index("probe") % SHARE).reshape(1)
    share_points = points // SHARE
    mine, other = call(
        local_body,
        [jax.ShapeDtypeStruct((probe_dev, share_points), jnp.float32)] * 2,
        [SMEM, SMEM, VMEM, VMEM, HBM, HBM],
        [pltpu.VMEM((near_local.shape[1] * LEAF_PTS, LEAF_PTS), jnp.bfloat16)] * 2
        + [pltpu.VMEM((2 * probe_dev, points), jnp.bfloat16), pltpu.SemaphoreType.DMA((2,))],
        micros=10.0,
    )(
        jnp.concatenate([(me * leaf_dev).reshape(1), side * (leaf_dev // SHARE)]),
        near_local, target, source, omega, omega_other,
    )
    bundles, distance, places = gather_bundles(sent, top, low, dests, [crossed[0], mine])
    relayed, raw = [], list(crossed)
    for i, part in enumerate(crossed):
        crossed[i] = after(part, relayed[-1]) if relayed else after(part, omega_beside, mine)
        relayed.append(exchange(crossed[i], "leaf", low))

    bundles = lax.optimization_barrier((*bundles, relayed[0], *raw[1:]))[: len(bundles)]
    pairs = jnp.stack([b[:, points:].astype(jnp.int32).reshape(2, pair_dev) for b in bundles])
    slots = (dests * 4 * CAP + BATCH - 1) // BATCH * BATCH
    codes = far_table(
        pairs, me, distance, places[0], top | low, leaf_dev, slots, dests * leaf_dev
    )
    far_source, far_target = features_of(
        points, 4, dests, places, bundles
    )
    owns, arrived = [], []
    for (first, size), from_across, from_both in zip(chunks, crossed, relayed):
        own, rest = call(
            functools.partial(far_body, first),
            [
                jax.ShapeDtypeStruct((size, points), jnp.float32),
                jax.ShapeDtypeStruct((dests - 1, size, points), jnp.bfloat16),
            ],
            [SMEM, VMEM, VMEM] + [HBM] * 4,
            [
                pltpu.VMEM((BATCH, LEAF_PTS, LEAF_PTS), jnp.bfloat16),
                pltpu.VMEM((size, dests * points + LEAF_PTS), jnp.float32),
                pltpu.VMEM((size, 4 * points), jnp.bfloat16),
                pltpu.SemaphoreType.DMA((4,)),
            ],
            micros=4.0,
        )(
            codes, far_source, far_target, omega, omega_beside, from_across, from_both
        )
        half = dests // 2
        while half > 1:
            got = exchange(rest[half - 1 :], "leaf", 2 * half)
            own = own + got[0].astype(jnp.float32)
            rest = rest[: half - 1] + got[1:]
            half //= 2
        owns.append(own)
        arrived.append(exchange(rest[0], "leaf", 2))
    theirs = exchange(other, "probe", 1)
    pick = call(
        pick_body,
        jax.ShapeDtypeStruct((parent_dev, SK2, CHILD * LEAF_PTS), jnp.bfloat16),
        [VMEM] * 2,
    )(skel_rows, parent_interp.transpose(0, 2, 1))
    near, merged, energy = call(
        functools.partial(merge_body, len(chunks)),
        [
            jax.ShapeDtypeStruct((probe_dev, points), jnp.float32),
            jax.ShapeDtypeStruct((probe_dev, parent_dev * SK2), jnp.float32),
            jax.ShapeDtypeStruct((parent_dev, LEAF_PTS), jnp.float32),
        ],
        [SMEM] + [VMEM] * (2 * len(chunks) + 3),
        micros=2.0,
    )(side, mine, theirs, *owns, *arrived, pick)
    n_probe = lax.axis_size("probe")
    if n_probe & (n_probe - 1):
        energies = [lax.psum(energy, "probe")]
    else:
        energies = [energy] + [exchange(energy, "probe", k) for k in range(1, n_probe)]
    parent = call(
        functools.partial(scale_body, float(SK2 * probe_dev * n_probe)),
        jax.ShapeDtypeStruct((probe_dev, parent_dev * SK2), jnp.float32),
        [VMEM] * (1 + len(energies)),
    )(merged, *energies)
    return near, parent


def solution(mesh):
    return jax.shard_map(
        per_device,
        mesh=mesh,
        in_specs=(
            P(None, "leaf"),
            P("leaf"),
            P("probe", "leaf"),
            P("leaf", None),
            P(None, "leaf"),
            P("leaf", None),
            P("leaf", None, None),
        ),
        out_specs=(P("probe", "leaf"), P("probe", "leaf")),
        check_vma=False,
    )
```

```python
import functools

import jax
import jax.numpy as jnp
from jax import lax
from jax.experimental import pallas as pl
from jax.experimental.pallas import tpu as pltpu
from jax.sharding import PartitionSpec as P

LEAF_PTS = 128
SK = 32
SK2 = 64
CHILD = 8
CAP = 16

DELTA_SQ = 0.0001
INV_FOUR_PI = 0.07957747154594767

VMEM_LIMIT = 12 * 1024 * 1024
BATCH = 24
FEATURES = 32
CHUNKS = (1, 1)
SHARE = 2

SMEM = pl.BlockSpec(memory_space=pltpu.SMEM)
VMEM = pl.BlockSpec(memory_space=pltpu.VMEM)
HBM = pl.BlockSpec(memory_space=pltpu.HBM)


def leaf_range(leaf):
    return pl.ds(pl.multiple_of(leaf * LEAF_PTS, LEAF_PTS), LEAF_PTS)


def split_three(values):
    first = values.astype(jnp.bfloat16).astype(jnp.float32)
    rest = values - first
    second = rest.astype(jnp.bfloat16).astype(jnp.float32)
    return first, second, rest - second


def six_products(left, right):
    a, b, c = split_three(left)
    p, q, r = split_three(right)
    return (a, a, b, b, a, c), (p, q, p, q, r, p)


def write_features(points_ref, rows, out, is_source):
    points = rows.shape[1]
    centred = points_ref[0:3, :points] - 0.5
    square = centred * centred
    norm = square[0:1] + square[1:2] + square[2:3]
    if is_source:
        root = 1.0 / (points_ref[3:4, :points] * INV_FOUR_PI)
        scale = root * root
        side, shared, last = 1, (centred * scale, scale), scale * (norm + DELTA_SQ)
    else:
        side, shared, last = 0, (-2.0 * centred, norm), None
    first = 0
    for values in shared:
        for part in six_products(values, values)[side]:
            rows[first : first + values.shape[0], :] = part
            first += values.shape[0]
    parts = [jnp.ones_like(norm)] * 3 if last is None else split_three(last)
    for part in parts:
        rows[first : first + 1, :] = part
        first += 1
    out[...] = rows[...].astype(jnp.bfloat16)


def feature_body(n_bundle, place_ref, *refs):
    source_ref, target_ref, rows = refs[n_bundle:]
    points = rows.shape[1]
    target_ref[:, target_ref.shape[1] - LEAF_PTS :] = jnp.ones((FEATURES, LEAF_PTS), jnp.bfloat16)
    rows[27:FEATURES, :] = jnp.zeros((FEATURES - 27, points), jnp.float32)
    for i in range(n_bundle):
        for kind, out_ref in enumerate((source_ref, target_ref)):
            place = place_ref[kind, i]

            @pl.when(place >= 0)
            def _(points_ref=refs[i], place=place, out_ref=out_ref, kind=kind):
                lanes = pl.ds(pl.multiple_of(place * points, LEAF_PTS), points)
                write_features(points_ref, rows, out_ref.at[:, lanes], kind == 0)


def far_prepare_body(n_bundle, outer, place_ref, *refs):
    source_ref, target_ref, table_ref, rows, inside_ref, values_ref, turned_ref = refs[n_bundle:]
    feature_body(n_bundle, place_ref, *refs[:n_bundle], source_ref, target_ref, rows)
    points = rows.shape[1]
    leaf_dev = points // LEAF_PTS
    shift = leaf_dev.bit_length() - 1
    spare = target_ref.shape[1] // LEAF_PTS - 1
    columns = refs[0].shape[1] - points
    inside_ref[...] = jnp.zeros_like(inside_ref)
    values_ref[...] = jnp.zeros_like(values_ref)
    me = place_ref[3, 0]
    for i in range(n_bundle):
        sender = place_ref[0, i]
        pairs = refs[i][:, points:]
        offset = ((me ^ place_ref[2, i]) - sender) * leaf_dev
        source = pairs[0:2] - offset.astype(jnp.float32)
        target = pairs[2:4].astype(jnp.int32)
        relation = lax.shift_right_logical(target, shift) ^ me
        owned = ((relation & outer) == 0) & (sender >= 0)
        member = lax.shift_right_logical(relation, 1) * leaf_dev + (target & (leaf_dev - 1))
        inside_ref[2 * i : 2 * i + 2, :columns] = owned.astype(jnp.float32)
        for h in range(2):
            values_ref[2 * i + h, 0:1, :columns] = source[h : h + 1]
            values_ref[2 * i + h, 1:2, :columns] = (member - spare)[h : h + 1].astype(jnp.float32)
    inside = inside_ref[...]
    count = inside.shape[0]

    def iota(shape, axis):
        return lax.broadcasted_iota(jnp.int32, shape, axis)

    def product(left, right):
        return jnp.dot(
            left.astype(jnp.bfloat16),
            right.astype(jnp.bfloat16),
            preferred_element_type=jnp.float32,
        )

    square, low = (LEAF_PTS, LEAF_PTS), (count, count)
    earlier = (iota(square, 0) < iota(square, 1)).astype(jnp.float32)
    above = (iota(low, 1) < iota(low, 0)).astype(jnp.float32)
    place = product(inside, earlier) + product(above, product(inside, jnp.ones(square)))
    turned_ref[...] = jnp.full(square, -1.0)
    turned_ref[:count, :] = jnp.where(inside > 0, place, -1.0)
    turned = jnp.transpose(turned_ref[...])
    length = table_ref.shape[1]
    wide = (length + LEAF_PTS - 1) // LEAF_PTS * LEAF_PTS
    slot = iota((LEAF_PTS, wide), 1).astype(jnp.float32)
    table = jnp.zeros((8, wide), jnp.float32)
    for r in range(2 * n_bundle):
        hit = (turned[:, r : r + 1] == slot).astype(jnp.float32)
        table = table + product(values_ref[r], hit)
    table_ref[...] = table[0:2, :length].astype(jnp.int32) + iota((2, length), 0) * spare


def turned_block(source, target):
    scaled = lax.dot_general(
        source, target, (((0,), (0,)), ((), ())), preferred_element_type=jnp.float32
    )
    return lax.rsqrt(scaled).astype(jnp.bfloat16)


def local_body(
    place_ref, near_ref, target_ref, source_ref, own_probes_ref, other_probes_ref,
    own_ref, other_ref, even_ref, odd_ref, omega_ref, sems,
):
    probe_dev = own_ref.shape[0]
    fetches = [
        pltpu.make_async_copy(
            ref, omega_ref.at[i * probe_dev : (i + 1) * probe_dev, :], sems.at[i]
        )
        for i, ref in enumerate((own_probes_ref, other_probes_ref))
    ]
    for fetch in fetches:
        fetch.start()
    entries = near_ref.shape[1]
    leaves = own_ref.shape[1] // LEAF_PTS
    offset, first = place_ref[0], place_ref[1]

    def source_of(t, e):
        return leaf_range(near_ref[first + t, e] - offset)

    def make(t, block_ref):
        target = target_ref[:, leaf_range(first + t)]
        for e in range(entries):
            block_ref[e * LEAF_PTS : (e + 1) * LEAF_PTS, :] = turned_block(
                source_ref[:, source_of(t, e)], target
            )

    def use(t, block_ref):
        probes = jnp.concatenate([omega_ref[:, source_of(t, e)] for e in range(entries)], axis=1)
        total = jnp.dot(probes, block_ref[...], preferred_element_type=jnp.float32)
        own_ref[:, leaf_range(t)] = total[:probe_dev]
        other_ref[:, leaf_range(t)] = total[probe_dev:]

    make(0, even_ref)
    for fetch in fetches:
        fetch.wait()

    def step(k, carry):
        make(2 * k + 1, odd_ref)
        use(2 * k, even_ref)
        make(jnp.minimum(2 * k + 2, leaves - 1), even_ref)
        use(2 * k + 1, odd_ref)
        return carry

    lax.fori_loop(0, leaves // 2, step, 0)


def far_body(first, table_ref, source_ref, target_ref, *refs):
    omegas = refs[:4]
    own_ref, rest_ref, block_ref, total_ref, omega_ref, sems = refs[4:]
    size, points = own_ref.shape
    fetches = []
    for k, slot in enumerate((0, 2, 1, 3)):
        rows = pl.ds(first if k < 2 else 0, size)
        fetches.append(
            pltpu.make_async_copy(
                omegas[k].at[rows, :],
                omega_ref.at[:, slot * points : (slot + 1) * points],
                sems.at[k],
            )
        )
        fetches[-1].start()
    total_ref[...] = jnp.zeros_like(total_ref)
    spare = total_ref.shape[1] // LEAF_PTS - 1
    rounds = sum(
        (table_ref[1, k] < spare).astype(jnp.int32) for k in range(0, table_ref.shape[1], BATCH)
    )
    for fetch in fetches:
        fetch.wait()

    def step(k, carry):
        for u in range(BATCH):
            item = k * BATCH + u
            block_ref[u] = turned_block(
                source_ref[:, leaf_range(table_ref[0, item])],
                target_ref[:, leaf_range(table_ref[1, item])],
            )
        for u in range(BATCH):
            item = k * BATCH + u
            product = jnp.dot(
                omega_ref[:, leaf_range(table_ref[0, item])],
                block_ref[u],
                preferred_element_type=jnp.float32,
            )
            total_ref[:, leaf_range(table_ref[1, item])] += product
        return carry

    lax.fori_loop(0, rounds, step, 0)
    own_ref[...] = total_ref[:, :points]
    for r in range(1, rest_ref.shape[0] + 1):
        rest_ref[r - 1] = total_ref[:, r * points : (r + 1) * points].astype(jnp.bfloat16)


def pick_body(skel_ref, interp_ref, out_ref):
    turned = jnp.transpose(skel_ref[...].astype(jnp.float32)).astype(jnp.int32)
    lane = lax.broadcasted_iota(jnp.int32, (SK, LEAF_PTS), 1)
    for leaf in range(skel_ref.shape[0]):
        parent, child = divmod(leaf, CHILD)
        chosen = (turned[:, leaf : leaf + 1] == lane).astype(jnp.float32).astype(jnp.bfloat16)
        out_ref[parent, :, child * LEAF_PTS : (child + 1) * LEAF_PTS] = jnp.dot(
            interp_ref[parent, :, child * SK : (child + 1) * SK],
            chosen,
            preferred_element_type=jnp.float32,
        ).astype(jnp.bfloat16)


def merge_body(n_chunk, side_ref, mine_ref, theirs_ref, *refs):
    owns, arrived = refs[:n_chunk], refs[n_chunk : 2 * n_chunk]
    pick_ref, near_ref, merged_ref, energy_ref = refs[2 * n_chunk :]
    width = mine_ref.shape[1]
    for half in range(SHARE):
        columns = slice(half * width, (half + 1) * width)
        first = 0
        for own_ref, arrived_ref in zip(owns, arrived):
            rows = slice(first, first + own_ref.shape[0])
            first += own_ref.shape[0]
            local = jnp.where(side_ref[0] == half, mine_ref[rows, :], theirs_ref[rows, :])
            near_ref[rows, columns] = (
                local + own_ref[:, columns] + arrived_ref[:, columns].astype(jnp.float32)
            )
    parents, _, width = pick_ref.shape
    for p in range(parents):
        merged = lax.dot_general(
            near_ref[:, p * width : (p + 1) * width].astype(jnp.bfloat16),
            pick_ref[p],
            (((1,), (1,)), ((), ())),
            preferred_element_type=jnp.float32,
        )
        merged_ref[:, p * SK2 : (p + 1) * SK2] = merged
        energy_ref[p : p + 1, :] = jnp.broadcast_to(
            jnp.sum(jnp.sum(merged * merged, axis=0, keepdims=True), axis=1, keepdims=True),
            (1, LEAF_PTS),
        )


def scale_body(count, merged_ref, *refs):
    energies, out_ref = refs[:-1], refs[-1]
    energy = sum(ref[...] for ref in energies[1:]) + energies[0][...]
    for p in range(energy.shape[0]):
        factor = lax.rsqrt(energy[p : p + 1, 0:SK2] / count + 1e-06)
        out_ref[:, p * SK2 : (p + 1) * SK2] = merged_ref[:, p * SK2 : (p + 1) * SK2] * factor


def call(body, out_shape, in_specs, scratch=(), micros=1.0):
    many = isinstance(out_shape, (tuple, list))
    return pl.pallas_call(
        body,
        out_shape=out_shape,
        in_specs=in_specs,
        out_specs=[VMEM] * len(out_shape) if many else VMEM,
        scratch_shapes=list(scratch),
        compiler_params=pltpu.CompilerParams(vmem_limit_bytes=VMEM_LIMIT),
        cost_estimate=pl.CostEstimate(
            flops=int(micros * 1e7), bytes_accessed=int(micros * 3e4), transcendentals=0
        ),
    )


def features_of(points, senders, dests, places, bundles, own=()):
    return call(
        functools.partial(feature_body, len(bundles)),
        [
            jax.ShapeDtypeStruct((FEATURES, senders * points), jnp.bfloat16),
            jax.ShapeDtypeStruct((FEATURES, dests * points + LEAF_PTS), jnp.bfloat16),
        ],
        [SMEM] + [VMEM] * (len(bundles) + len(own)),
        [pltpu.VMEM((FEATURES, points), jnp.float32)],
    )(places, *bundles, *own)


def exchange(array, axis, bit):
    size = lax.axis_size(axis)
    return lax.ppermute(array, axis, [(i, i ^ bit) for i in range(size)])


def after(array, *others):
    return lax.optimization_barrier((array, *others))[0]


def gather_bundles(sent, top, low, dests, wait):
    masks = [top, low, top | low] + [2 * r for r in range(1, dests)]
    n_leaf, n_probe = lax.axis_size("leaf"), lax.axis_size("probe")
    if len(masks) != 4 or n_probe % 2:
        rank = jnp.arange(len(masks), dtype=jnp.int32)
        bundles = [exchange(sent, "leaf", mask) for mask in masks]
    else:
        core = lax.axis_index("probe") % 2
        rank = jnp.stack([core, 2 + core, 1 - core, 3 - core])
        bundles = []
        for half in (0, 2):
            pairs = [
                (i * n_probe + q, (i ^ masks[half + q % 2]) * n_probe + q)
                for i in range(n_leaf)
                for q in range(n_probe)
            ]
            bundles.append(lax.ppermute(sent, ("leaf", "probe"), pairs))
        bundles = list(lax.optimization_barrier((*bundles, *wait))[:2])
        bundles += [exchange(bundle, "probe", 1) for bundle in bundles]
    distance = jnp.where(
        rank < 3, (rank + 1) % 2 * top + (rank + 1) // 2 % 2 * low, 2 * (rank - 2)
    )
    distance = jnp.where(rank == 2, top | low, distance)
    sender = jnp.where(rank < 3, rank + 1, -1)
    member = jnp.where(rank < 3, -1, rank - 2)
    zero = jnp.zeros((1,), jnp.int32)
    return (
        [sent, *bundles],
        jnp.concatenate([zero, distance]),
        jnp.stack([jnp.concatenate([zero, sender]), jnp.concatenate([zero, member])]),
    )


def per_device(coords, weights, omega, near_local, far_pairs, skel_rows, parent_interp):
    n_leaf = lax.axis_size("leaf")
    points = coords.shape[1]
    leaf_dev = points // LEAF_PTS
    probe_dev = omega.shape[0]
    parent_dev = leaf_dev // CHILD
    me = lax.axis_index("leaf")
    top, low = n_leaf // 2, 1
    dests = n_leaf // 4
    pair_dev = far_pairs.shape[1]
    unit = probe_dev // sum(CHUNKS)
    chunks = [(unit * sum(CHUNKS[:i]), unit * c) for i, c in enumerate(CHUNKS)]

    omega_other = exchange(omega, "probe", 1)
    parts = lax.optimization_barrier([omega[first : first + size] for first, size in chunks])
    crossed = [exchange(part, "leaf", top) for part in parts]
    coords = after(coords, *parts)
    omega_beside = exchange(after(omega, *parts), "leaf", low)
    pair_columns = 2 * pair_dev // 4
    sent = jnp.concatenate(
        [
            jnp.concatenate([coords, weights[None]], axis=0),
            far_pairs.reshape(4, pair_columns).astype(jnp.float32),
        ],
        axis=1,
    )
    source, target = features_of(points, 1, 1, jnp.zeros((2, 1), jnp.int32), [sent])
    side = (lax.axis_index("probe") % SHARE).reshape(1)
    share_points = points // SHARE
    mine, other = call(
        local_body,
        [jax.ShapeDtypeStruct((probe_dev, share_points), jnp.float32)] * 2,
        [SMEM, SMEM, VMEM, VMEM, HBM, HBM],
        [pltpu.VMEM((near_local.shape[1] * LEAF_PTS, LEAF_PTS), jnp.bfloat16)] * 2
        + [pltpu.VMEM((2 * probe_dev, points), jnp.bfloat16), pltpu.SemaphoreType.DMA((2,))],
        micros=10.0,
    )(
        jnp.concatenate([(me * leaf_dev).reshape(1), side * (leaf_dev // SHARE)]),
        near_local, target, source, omega, omega_other,
    )
    bundles, distance, places = gather_bundles(sent, top, low, dests, [crossed[0], mine])
    crossed[0] = after(crossed[0], omega_beside, mine)
    relayed = [exchange(crossed[0], "leaf", low)]
    slots = (dests * 4 * CAP + BATCH - 1) // BATCH * BATCH
    n_rows = (2 * len(bundles) + 7) // 8 * 8
    far_source, far_target, codes = call(
        functools.partial(far_prepare_body, len(bundles), top | low),
        [
            jax.ShapeDtypeStruct((FEATURES, 4 * points), jnp.bfloat16),
            jax.ShapeDtypeStruct((FEATURES, dests * points + LEAF_PTS), jnp.bfloat16),
            jax.ShapeDtypeStruct((2, slots), jnp.int32),
        ],
        [SMEM] + [VMEM] * len(bundles),
        [
            pltpu.VMEM((FEATURES, points), jnp.float32),
            pltpu.VMEM((n_rows, LEAF_PTS), jnp.float32),
            pltpu.VMEM((n_rows, 8, LEAF_PTS), jnp.float32),
            pltpu.VMEM((LEAF_PTS, LEAF_PTS), jnp.float32),
        ],
    )(
        jnp.concatenate([places, distance[None], jnp.broadcast_to(me, (1, len(bundles)))]),
        *bundles,
    )
    for i, part in enumerate(crossed[1:], 1):
        crossed[i] = after(part, relayed[-1], codes)
        relayed.append(exchange(crossed[i], "leaf", low))
    owns, arrived = [], []
    for (first, size), from_across, from_both in zip(chunks, crossed, relayed):
        own, rest = call(
            functools.partial(far_body, first),
            [
                jax.ShapeDtypeStruct((size, points), jnp.float32),
                jax.ShapeDtypeStruct((dests - 1, size, points), jnp.bfloat16),
            ],
            [SMEM, VMEM, VMEM] + [HBM] * 4,
            [
                pltpu.VMEM((BATCH, LEAF_PTS, LEAF_PTS), jnp.bfloat16),
                pltpu.VMEM((size, dests * points + LEAF_PTS), jnp.float32),
                pltpu.VMEM((size, 4 * points), jnp.bfloat16),
                pltpu.SemaphoreType.DMA((4,)),
            ],
            micros=4.0,
        )(
            codes, far_source, far_target, omega, omega_beside, from_across, from_both
        )
        half = dests // 2
        while half > 1:
            got = exchange(rest[half - 1 :], "leaf", 2 * half)
            own = own + got[0].astype(jnp.float32)
            rest = rest[: half - 1] + got[1:]
            half //= 2
        owns.append(own)
        arrived.append(exchange(rest[0], "leaf", 2))
    theirs = exchange(other, "probe", 1)
    pick = call(
        pick_body,
        jax.ShapeDtypeStruct((parent_dev, SK2, CHILD * LEAF_PTS), jnp.bfloat16),
        [VMEM] * 2,
    )(skel_rows, parent_interp.transpose(0, 2, 1))
    near, merged, energy = call(
        functools.partial(merge_body, len(chunks)),
        [
            jax.ShapeDtypeStruct((probe_dev, points), jnp.float32),
            jax.ShapeDtypeStruct((probe_dev, parent_dev * SK2), jnp.float32),
            jax.ShapeDtypeStruct((parent_dev, LEAF_PTS), jnp.float32),
        ],
        [SMEM] + [VMEM] * (2 * len(chunks) + 3),
        micros=2.0,
    )(side, mine, theirs, *owns, *arrived, pick)
    n_probe = lax.axis_size("probe")
    if n_probe & (n_probe - 1):
        energies = [lax.psum(energy, "probe")]
    else:
        energies = [energy] + [exchange(energy, "probe", k) for k in range(1, n_probe)]
    parent = call(
        functools.partial(scale_body, float(SK2 * probe_dev * n_probe)),
        jax.ShapeDtypeStruct((probe_dev, parent_dev * SK2), jnp.float32),
        [VMEM] * (1 + len(energies)),
    )(merged, *energies)
    return near, parent


def solution(mesh):
    return jax.shard_map(
        per_device,
        mesh=mesh,
        in_specs=(
            P(None, "leaf"),
            P("leaf"),
            P("probe", "leaf"),
            P("leaf", None),
            P(None, "leaf"),
            P("leaf", None),
            P("leaf", None, None),
        ),
        out_specs=(P("probe", "leaf"), P("probe", "leaf")),
        check_vma=False,
    )
```

```python
import functools

import jax
import jax.numpy as jnp
from jax import lax
from jax.experimental import pallas as pl
from jax.experimental.pallas import tpu as pltpu
from jax.sharding import PartitionSpec as P

LEAF_PTS = 128
SK = 32
SK2 = 64
CHILD = 8
CAP = 16

DELTA_SQ = 0.0001
INV_FOUR_PI = 0.07957747154594767

VMEM_LIMIT = 12 * 1024 * 1024
BATCH = 24
FEATURES = 32
CHUNKS = (1, 1)
SHARE = 2

SMEM = pl.BlockSpec(memory_space=pltpu.SMEM)
VMEM = pl.BlockSpec(memory_space=pltpu.VMEM)
HBM = pl.BlockSpec(memory_space=pltpu.HBM)


def leaf_range(leaf):
    return pl.ds(pl.multiple_of(leaf * LEAF_PTS, LEAF_PTS), LEAF_PTS)


def split_three(values):
    first = values.astype(jnp.bfloat16).astype(jnp.float32)
    rest = values - first
    second = rest.astype(jnp.bfloat16).astype(jnp.float32)
    return first, second, rest - second


def six_products(left, right):
    a, b, c = split_three(left)
    p, q, r = split_three(right)
    return (a, a, b, b, a, c), (p, q, p, q, r, p)


def write_features(points_ref, rows, out, is_source):
    points = rows.shape[1]
    centred = points_ref[0:3, :points] - 0.5
    square = centred * centred
    norm = square[0:1] + square[1:2] + square[2:3]
    if is_source:
        root = 1.0 / (points_ref[3:4, :points] * INV_FOUR_PI)
        scale = root * root
        side, shared, last = 1, (centred * scale, scale), scale * (norm + DELTA_SQ)
    else:
        side, shared, last = 0, (-2.0 * centred, norm), None
    first = 0
    for values in shared:
        for part in six_products(values, values)[side]:
            rows[first : first + values.shape[0], :] = part
            first += values.shape[0]
    parts = [jnp.ones_like(norm)] * 3 if last is None else split_three(last)
    for part in parts:
        rows[first : first + 1, :] = part
        first += 1
    out[...] = rows[...].astype(jnp.bfloat16)


def feature_body(n_bundle, place_ref, *refs):
    source_ref, target_ref, rows = refs[n_bundle:]
    points = rows.shape[1]
    target_ref[:, target_ref.shape[1] - LEAF_PTS :] = jnp.ones((FEATURES, LEAF_PTS), jnp.bfloat16)
    rows[27:FEATURES, :] = jnp.zeros((FEATURES - 27, points), jnp.float32)
    for i in range(n_bundle):
        for kind, out_ref in enumerate((source_ref, target_ref)):
            place = place_ref[kind, i]

            @pl.when(place >= 0)
            def _(points_ref=refs[i], place=place, out_ref=out_ref, kind=kind):
                lanes = pl.ds(pl.multiple_of(place * points, LEAF_PTS), points)
                write_features(points_ref, rows, out_ref.at[:, lanes], kind == 0)


def far_prepare_body(n_bundle, outer, place_ref, *refs):
    source_ref, target_ref, table_ref, rows, inside_ref, values_ref, turned_ref = refs[n_bundle:]
    feature_body(n_bundle, place_ref, *refs[:n_bundle], source_ref, target_ref, rows)
    points = rows.shape[1]
    leaf_dev = points // LEAF_PTS
    shift = leaf_dev.bit_length() - 1
    spare = target_ref.shape[1] // LEAF_PTS - 1
    columns = refs[0].shape[1] - points
    inside_ref[...] = jnp.zeros_like(inside_ref)
    values_ref[...] = jnp.zeros_like(values_ref)
    me = place_ref[3, 0]
    for i in range(n_bundle):
        sender = place_ref[0, i]
        pairs = refs[i][:, points:]
        offset = ((me ^ place_ref[2, i]) - sender) * leaf_dev
        source = pairs[0:2] - offset.astype(jnp.float32)
        target = pairs[2:4].astype(jnp.int32)
        relation = lax.shift_right_logical(target, shift) ^ me
        owned = ((relation & outer) == 0) & (sender >= 0)
        member = lax.shift_right_logical(relation, 1) * leaf_dev + (target & (leaf_dev - 1))
        inside_ref[2 * i : 2 * i + 2, :columns] = owned.astype(jnp.float32)
        for h in range(2):
            values_ref[2 * i + h, 0:1, :columns] = source[h : h + 1]
            values_ref[2 * i + h, 1:2, :columns] = (member - spare)[h : h + 1].astype(jnp.float32)
    inside = inside_ref[...]
    count = inside.shape[0]

    def iota(shape, axis):
        return lax.broadcasted_iota(jnp.int32, shape, axis)

    def product(left, right):
        return jnp.dot(
            left.astype(jnp.bfloat16),
            right.astype(jnp.bfloat16),
            preferred_element_type=jnp.float32,
        )

    square, low = (LEAF_PTS, LEAF_PTS), (count, count)
    earlier = (iota(square, 0) < iota(square, 1)).astype(jnp.float32)
    above = (iota(low, 1) < iota(low, 0)).astype(jnp.float32)
    place = product(inside, earlier) + product(above, product(inside, jnp.ones(square)))
    turned_ref[...] = jnp.full(square, -1.0)
    turned_ref[:count, :] = jnp.where(inside > 0, place, -1.0)
    turned = jnp.transpose(turned_ref[...])
    length = table_ref.shape[1]
    wide = (length + LEAF_PTS - 1) // LEAF_PTS * LEAF_PTS
    slot = iota((LEAF_PTS, wide), 1).astype(jnp.float32)
    table = jnp.zeros((8, wide), jnp.float32)
    for r in range(2 * n_bundle):
        hit = (turned[:, r : r + 1] == slot).astype(jnp.float32)
        table = table + product(values_ref[r], hit)
    table_ref[...] = table[0:2, :length].astype(jnp.int32) + iota((2, length), 0) * spare


def turned_block(source, target):
    scaled = lax.dot_general(
        source, target, (((0,), (0,)), ((), ())), preferred_element_type=jnp.float32
    )
    return lax.rsqrt(scaled).astype(jnp.bfloat16)


def local_body(
    place_ref, near_ref, target_ref, source_ref, own_probes_ref, other_probes_ref,
    own_ref, other_ref, even_ref, odd_ref, omega_ref, sems,
):
    probe_dev = own_ref.shape[0]
    fetches = [
        pltpu.make_async_copy(
            ref, omega_ref.at[i * probe_dev : (i + 1) * probe_dev, :], sems.at[i]
        )
        for i, ref in enumerate((own_probes_ref, other_probes_ref))
    ]
    for fetch in fetches:
        fetch.start()
    entries = near_ref.shape[1]
    leaves = own_ref.shape[1] // LEAF_PTS
    offset, first = place_ref[0], place_ref[1]

    def source_of(t, e):
        return leaf_range(near_ref[first + t, e] - offset)

    def make(t, block_ref):
        target = target_ref[:, leaf_range(first + t)]
        for e in range(entries):
            block_ref[e * LEAF_PTS : (e + 1) * LEAF_PTS, :] = turned_block(
                source_ref[:, source_of(t, e)], target
            )

    def use(t, block_ref):
        probes = jnp.concatenate([omega_ref[:, source_of(t, e)] for e in range(entries)], axis=1)
        total = jnp.dot(probes, block_ref[...], preferred_element_type=jnp.float32)
        own_ref[:, leaf_range(t)] = total[:probe_dev]
        other_ref[:, leaf_range(t)] = total[probe_dev:]

    make(0, even_ref)
    for fetch in fetches:
        fetch.wait()

    def step(k, carry):
        make(2 * k + 1, odd_ref)
        use(2 * k, even_ref)
        make(jnp.minimum(2 * k + 2, leaves - 1), even_ref)
        use(2 * k + 1, odd_ref)
        return carry

    lax.fori_loop(0, leaves // 2, step, 0)


def far_body(first, table_ref, source_ref, target_ref, *refs):
    omegas = refs[:4]
    own_ref, rest_ref, block_ref, total_ref, omega_ref, sems = refs[4:]
    size, points = own_ref.shape
    fetches = []
    for k, slot in enumerate((0, 2, 1, 3)):
        rows = pl.ds(first if k < 2 else 0, size)
        fetches.append(
            pltpu.make_async_copy(
                omegas[k].at[rows, :],
                omega_ref.at[:, slot * points : (slot + 1) * points],
                sems.at[k],
            )
        )
        fetches[-1].start()
    total_ref[...] = jnp.zeros_like(total_ref)
    spare = total_ref.shape[1] // LEAF_PTS - 1
    rounds = sum(
        (table_ref[1, k] < spare).astype(jnp.int32) for k in range(0, table_ref.shape[1], BATCH)
    )
    for fetch in fetches:
        fetch.wait()

    def step(k, carry):
        for u in range(BATCH):
            item = k * BATCH + u
            block_ref[u] = turned_block(
                source_ref[:, leaf_range(table_ref[0, item])],
                target_ref[:, leaf_range(table_ref[1, item])],
            )
        for u in range(BATCH):
            item = k * BATCH + u
            product = jnp.dot(
                omega_ref[:, leaf_range(table_ref[0, item])],
                block_ref[u],
                preferred_element_type=jnp.float32,
            )
            total_ref[:, leaf_range(table_ref[1, item])] += product
        return carry

    lax.fori_loop(0, rounds, step, 0)
    own_ref[...] = total_ref[:, :points]
    for r in range(1, rest_ref.shape[0] + 1):
        rest_ref[r - 1] = total_ref[:, r * points : (r + 1) * points].astype(jnp.bfloat16)


def pick_body(skel_ref, interp_ref, out_ref):
    turned = jnp.transpose(skel_ref[...].astype(jnp.float32)).astype(jnp.int32)
    lane = lax.broadcasted_iota(jnp.int32, (SK, LEAF_PTS), 1)
    for leaf in range(skel_ref.shape[0]):
        parent, child = divmod(leaf, CHILD)
        chosen = (turned[:, leaf : leaf + 1] == lane).astype(jnp.float32).astype(jnp.bfloat16)
        out_ref[parent, :, child * LEAF_PTS : (child + 1) * LEAF_PTS] = jnp.dot(
            interp_ref[parent, :, child * SK : (child + 1) * SK],
            chosen,
            preferred_element_type=jnp.float32,
        ).astype(jnp.bfloat16)


def merge_body(n_chunk, side_ref, mine_ref, theirs_ref, *refs):
    owns, arrived = refs[:n_chunk], refs[n_chunk : 2 * n_chunk]
    pick_ref, merged_ref, energy_ref, near_ref = refs[2 * n_chunk :]
    width = mine_ref.shape[1]
    for half in range(SHARE):
        columns = slice(half * width, (half + 1) * width)
        first = 0
        for own_ref, arrived_ref in zip(owns, arrived):
            rows = slice(first, first + own_ref.shape[0])
            first += own_ref.shape[0]
            local = jnp.where(side_ref[0] == half, mine_ref[rows, :], theirs_ref[rows, :])
            near_ref[rows, columns] = (
                local + own_ref[:, columns] + arrived_ref[:, columns].astype(jnp.float32)
            )
    parents, _, width = pick_ref.shape
    for p in range(parents):
        merged = lax.dot_general(
            near_ref[:, p * width : (p + 1) * width].astype(jnp.bfloat16),
            pick_ref[p],
            (((1,), (1,)), ((), ())),
            preferred_element_type=jnp.float32,
        )
        merged_ref[:, p * SK2 : (p + 1) * SK2] = merged
        energy_ref[p : p + 1, :] = jnp.broadcast_to(
            jnp.sum(jnp.sum(merged * merged, axis=0, keepdims=True), axis=1, keepdims=True),
            (1, LEAF_PTS),
        )


def near_rows(half, rows, side_ref, mine_ref, theirs_ref, own_ref, arrived_ref):
    width = mine_ref.shape[1]
    columns = slice(half * width, (half + 1) * width)
    local = jnp.where(side_ref[0] == half, mine_ref[rows, :], theirs_ref[rows, :])
    return local + own_ref[:, columns] + arrived_ref[:, columns].astype(jnp.float32)


def near_body(n_chunk, side_ref, mine_ref, theirs_ref, *refs):
    owns, arrived, near_ref = refs[:n_chunk], refs[n_chunk : 2 * n_chunk], refs[-1]
    width = mine_ref.shape[1]
    for half in range(SHARE):
        first = 0
        for own_ref, arrived_ref in zip(owns, arrived):
            rows = slice(first, first + own_ref.shape[0])
            first += own_ref.shape[0]
            near_ref[rows, half * width : (half + 1) * width] = near_rows(
                half, rows, side_ref, mine_ref, theirs_ref, own_ref, arrived_ref
            )


def scale_body(count, merged_ref, *refs):
    energies, out_ref = refs[:-1], refs[-1]
    energy = sum(ref[...] for ref in energies[1:]) + energies[0][...]
    for p in range(energy.shape[0]):
        factor = lax.rsqrt(energy[p : p + 1, 0:SK2] / count + 1e-06)
        out_ref[:, p * SK2 : (p + 1) * SK2] = merged_ref[:, p * SK2 : (p + 1) * SK2] * factor


def call(body, out_shape, in_specs, scratch=(), micros=1.0):
    many = isinstance(out_shape, (tuple, list))
    return pl.pallas_call(
        body,
        out_shape=out_shape,
        in_specs=in_specs,
        out_specs=[VMEM] * len(out_shape) if many else VMEM,
        scratch_shapes=list(scratch),
        compiler_params=pltpu.CompilerParams(vmem_limit_bytes=VMEM_LIMIT),
        cost_estimate=pl.CostEstimate(
            flops=int(micros * 1e7), bytes_accessed=int(micros * 3e4), transcendentals=0
        ),
    )


def features_of(points, senders, dests, places, bundles, own=()):
    return call(
        functools.partial(feature_body, len(bundles)),
        [
            jax.ShapeDtypeStruct((FEATURES, senders * points), jnp.bfloat16),
            jax.ShapeDtypeStruct((FEATURES, dests * points + LEAF_PTS), jnp.bfloat16),
        ],
        [SMEM] + [VMEM] * (len(bundles) + len(own)),
        [pltpu.VMEM((FEATURES, points), jnp.float32)],
    )(places, *bundles, *own)


def exchange(array, axis, bit):
    size = lax.axis_size(axis)
    return lax.ppermute(array, axis, [(i, i ^ bit) for i in range(size)])


def after(array, *others):
    return lax.optimization_barrier((array, *others))[0]


def gather_bundles(sent, top, low, dests, wait):
    masks = [top, low, top | low] + [2 * r for r in range(1, dests)]
    n_leaf, n_probe = lax.axis_size("leaf"), lax.axis_size("probe")
    if len(masks) != 4 or n_probe % 2:
        rank = jnp.arange(len(masks), dtype=jnp.int32)
        bundles = [exchange(sent, "leaf", mask) for mask in masks]
    else:
        core = lax.axis_index("probe") % 2
        rank = jnp.stack([core, 2 + core, 1 - core, 3 - core])
        bundles = []
        for half in (0, 2):
            pairs = [
                (i * n_probe + q, (i ^ masks[half + q % 2]) * n_probe + q)
                for i in range(n_leaf)
                for q in range(n_probe)
            ]
            bundles.append(lax.ppermute(sent, ("leaf", "probe"), pairs))
        bundles = list(lax.optimization_barrier((*bundles, *wait))[:2])
        bundles += [exchange(bundle, "probe", 1) for bundle in bundles]
    distance = jnp.where(
        rank < 3, (rank + 1) % 2 * top + (rank + 1) // 2 % 2 * low, 2 * (rank - 2)
    )
    distance = jnp.where(rank == 2, top | low, distance)
    sender = jnp.where(rank < 3, rank + 1, -1)
    member = jnp.where(rank < 3, -1, rank - 2)
    zero = jnp.zeros((1,), jnp.int32)
    return (
        [sent, *bundles],
        jnp.concatenate([zero, distance]),
        jnp.stack([jnp.concatenate([zero, sender]), jnp.concatenate([zero, member])]),
    )


def per_device(coords, weights, omega, near_local, far_pairs, skel_rows, parent_interp):
    n_leaf = lax.axis_size("leaf")
    points = coords.shape[1]
    leaf_dev = points // LEAF_PTS
    probe_dev = omega.shape[0]
    parent_dev = leaf_dev // CHILD
    me = lax.axis_index("leaf")
    top, low = n_leaf // 2, 1
    dests = n_leaf // 4
    pair_dev = far_pairs.shape[1]
    unit = probe_dev // sum(CHUNKS)
    chunks = [(unit * sum(CHUNKS[:i]), unit * c) for i, c in enumerate(CHUNKS)]

    omega_other = exchange(omega, "probe", 1)
    parts = lax.optimization_barrier([omega[first : first + size] for first, size in chunks])
    crossed = [exchange(part, "leaf", top) for part in parts]
    coords = after(coords, *parts)
    omega_beside = exchange(after(omega, *parts), "leaf", low)
    pair_columns = 2 * pair_dev // 4
    sent = jnp.concatenate(
        [
            jnp.concatenate([coords, weights[None]], axis=0),
            far_pairs.reshape(4, pair_columns).astype(jnp.float32),
        ],
        axis=1,
    )
    source, target = features_of(points, 1, 1, jnp.zeros((2, 1), jnp.int32), [sent])
    side = (lax.axis_index("probe") % SHARE).reshape(1)
    share_points = points // SHARE
    mine, other = call(
        local_body,
        [jax.ShapeDtypeStruct((probe_dev, share_points), jnp.float32)] * 2,
        [SMEM, SMEM, VMEM, VMEM, HBM, HBM],
        [pltpu.VMEM((near_local.shape[1] * LEAF_PTS, LEAF_PTS), jnp.bfloat16)] * 2
        + [pltpu.VMEM((2 * probe_dev, points), jnp.bfloat16), pltpu.SemaphoreType.DMA((2,))],
        micros=10.0,
    )(
        jnp.concatenate([(me * leaf_dev).reshape(1), side * (leaf_dev // SHARE)]),
        near_local, target, source, omega, omega_other,
    )
    bundles, distance, places = gather_bundles(sent, top, low, dests, [crossed[0], mine])
    crossed[0] = after(crossed[0], omega_beside, mine)
    relayed = [exchange(crossed[0], "leaf", low)]
    slots = (dests * 4 * CAP + BATCH - 1) // BATCH * BATCH
    n_rows = (2 * len(bundles) + 7) // 8 * 8
    far_source, far_target, codes = call(
        functools.partial(far_prepare_body, len(bundles), top | low),
        [
            jax.ShapeDtypeStruct((FEATURES, 4 * points), jnp.bfloat16),
            jax.ShapeDtypeStruct((FEATURES, dests * points + LEAF_PTS), jnp.bfloat16),
            jax.ShapeDtypeStruct((2, slots), jnp.int32),
        ],
        [SMEM] + [VMEM] * len(bundles),
        [
            pltpu.VMEM((FEATURES, points), jnp.float32),
            pltpu.VMEM((n_rows, LEAF_PTS), jnp.float32),
            pltpu.VMEM((n_rows, 8, LEAF_PTS), jnp.float32),
            pltpu.VMEM((LEAF_PTS, LEAF_PTS), jnp.float32),
        ],
    )(
        jnp.concatenate([places, distance[None], jnp.broadcast_to(me, (1, len(bundles)))]),
        *bundles,
    )
    for i, part in enumerate(crossed[1:], 1):
        crossed[i] = after(part, relayed[-1], codes)
        relayed.append(exchange(crossed[i], "leaf", low))
    owns, arrived = [], []
    for (first, size), from_across, from_both in zip(chunks, crossed, relayed):
        own, rest = call(
            functools.partial(far_body, first),
            [
                jax.ShapeDtypeStruct((size, points), jnp.float32),
                jax.ShapeDtypeStruct((dests - 1, size, points), jnp.bfloat16),
            ],
            [SMEM, VMEM, VMEM] + [HBM] * 4,
            [
                pltpu.VMEM((BATCH, LEAF_PTS, LEAF_PTS), jnp.bfloat16),
                pltpu.VMEM((size, dests * points + LEAF_PTS), jnp.float32),
                pltpu.VMEM((size, 4 * points), jnp.bfloat16),
                pltpu.SemaphoreType.DMA((4,)),
            ],
            micros=4.0,
        )(
            codes, far_source, far_target, omega, omega_beside, from_across, from_both
        )
        half = dests // 2
        while half > 1:
            got = exchange(rest[half - 1 :], "leaf", 2 * half)
            own = own + got[0].astype(jnp.float32)
            rest = rest[: half - 1] + got[1:]
            half //= 2
        owns.append(own)
        arrived.append(exchange(rest[0], "leaf", 2))
    theirs = exchange(other, "probe", 1)
    pick = call(
        pick_body,
        jax.ShapeDtypeStruct((parent_dev, SK2, CHILD * LEAF_PTS), jnp.bfloat16),
        [VMEM] * 2,
    )(skel_rows, parent_interp.transpose(0, 2, 1))
    merged, energy = call(
        functools.partial(merge_body, len(chunks)),
        [
            jax.ShapeDtypeStruct((probe_dev, parent_dev * SK2), jnp.float32),
            jax.ShapeDtypeStruct((parent_dev, LEAF_PTS), jnp.float32),
        ],
        [SMEM] + [VMEM] * (2 * len(chunks) + 3),
        [pltpu.VMEM((probe_dev, points), jnp.float32)],
        micros=2.0,
    )(side, mine, theirs, *owns, *arrived, pick)
    near = call(
        functools.partial(near_body, len(chunks)),
        jax.ShapeDtypeStruct((probe_dev, points), jnp.float32),
        [SMEM] + [VMEM] * (2 + 2 * len(chunks)),
    )(side, mine, theirs, *owns, *arrived)
    n_probe = lax.axis_size("probe")
    if n_probe & (n_probe - 1):
        energies = [lax.psum(energy, "probe")]
    else:
        energies = [energy] + [exchange(energy, "probe", k) for k in range(1, n_probe)]
    near, merged = lax.optimization_barrier((near, merged))
    parent = call(
        functools.partial(scale_body, float(SK2 * probe_dev * n_probe)),
        jax.ShapeDtypeStruct((probe_dev, parent_dev * SK2), jnp.float32),
        [VMEM] * (1 + len(energies)),
    )(merged, *energies)
    return near, parent


def solution(mesh):
    return jax.shard_map(
        per_device,
        mesh=mesh,
        in_specs=(
            P(None, "leaf"),
            P("leaf"),
            P("probe", "leaf"),
            P("leaf", None),
            P(None, "leaf"),
            P("leaf", None),
            P("leaf", None, None),
        ),
        out_specs=(P("probe", "leaf"), P("probe", "leaf")),
        check_vma=False,
    )
```
